128 devices in a mesh: gz: 2 (over x_lo), row: 8 (over y, core), col: 8 (over x_hi, z).
Axes of the slice: x: 4 (x_hi: 2, x_lo: 2; x = x_hi * 2 + x_lo), y: 4, z: 4, core: 2. Of those that a mesh axis runs over, the one named last changes fastest.
Arguments:
- anc_inverse: float32 [8192, 8192], P(('gz', 'row'), 'col'), may hold values from -0.25 to 0.25
- row_blocks: int32 [2, 8], replicated, may hold values from 0 to 31, as said below
- panel: float32 [2, 2048, 6144], P('gz', 'row', 'col'), may hold values from -1 to 1
- diag_inverse: float32 [2, 6144, 6144], P('gz', 'row', 'col'), may hold values from -6 to 6
Outputs:
- panel_inverse: float32 [2, 2048, 6144], P('gz', 'row', 'col')
- child_inverse: float32 [2, 6144, 6144], P('gz', 'row', 'col')
The draws below stay inside these ranges and needn't reach their ends.
Inputs may be any that keep to these rules, and one draw needn't show every extreme that they name: `row_blocks`: entry k of a child's list is one of 2 * k, 2 * k + 1, 2 * 8 + 2 * k, 2 * 8 + 2 * k + 1; of entries 2 * m and 2 * m + 1 exactly one is 16 or more, so that the entries of one list divided by 4 and rounded down are all different. The first child's list begins with 0 and ends with 31.
All inputs are finite; a program needn't handle non-finite values.
Results may differ from the reference program's by a relative error of at most 0.0001.
Values sent between devices are 32-bit elements; how exact they have to be, the bound alone decides.
No kernel may reach another device: no remote copies, remote signals or barrier semaphores. Data moves between devices by JAX's collectives and lax.ppermute only.
A program may use at most 128 MiB of HBM per device.

```python
import jax
import jax.numpy as jnp
from jax import lax

BS = 256
CH = 6144
GRID = 8
KIDS = 2
SEP = 8192
RSEL = 2048


def draw_row_blocks(key, part):
    key = jax.random.fold_in(key, 11)
    first_key, second_key = jax.random.split(key)
    upper_bits = jax.random.randint(first_key, (KIDS, GRID // 2, 1), 0, 2)
    upper_bits = upper_bits.at[0, 0, 0].set(0).at[0, GRID // 2 - 1, 0].set(0)
    high_bits = jnp.concatenate([upper_bits, 1 - upper_bits], axis=2).reshape(KIDS, GRID)
    low_bits = jax.random.randint(second_key, (KIDS, GRID), 0, 2)
    low_bits = low_bits.at[0, 0].set(0).at[0, GRID - 1].set(1)
    positions = jnp.arange(GRID, dtype=jnp.int32)[None, :]
    return (2 * positions + low_bits + 2 * GRID * high_bits).astype(jnp.int32)


def block_levels(key, extent, cuts, least, top_value):
    loudness = 1.0
    for dim, shards_of in cuts:
        draws = jax.random.uniform(jax.random.fold_in(jax.random.fold_in(key, 6), dim), (shards_of,), jnp.float32, least / len(cuts), top_value / len(cuts))
        loudness = loudness * jnp.repeat(jnp.exp(draws), extent[dim] // shards_of).reshape((-1,) + (1,) * (len(extent) - 1 - dim))
    return loudness


def scatter_about(own_key, shape, scale, bound, cuts=(), kind=jnp.bfloat16):
    entries = jax.random.normal(own_key, shape, jnp.float32) * scale
    if len(cuts) > 0:
        entries = block_levels(own_key, shape, cuts, -0.22, 0.18) * entries
    return jnp.clip(entries, min=-bound, max=bound).astype(kind)


def setup_inputs(seed: int = 0) -> dict:
    splits = jax.random.split(jax.random.key(seed), 5)
    return {
        "anc_inverse": scatter_about(splits[0], (SEP, SEP), (RSEL // 4) ** -0.5, 0.25, ((0, 16), (1, 8)), jnp.float32),
        "row_blocks": draw_row_blocks(jax.random.fold_in(splits[4], 71), 0),
        "panel": scatter_about(splits[2], (KIDS, RSEL, CH), (max(RSEL // 64, 1)) ** -0.5, 1.0, ((0, 2), (1, 8), (2, 8)), jnp.float32),
        "diag_inverse": scatter_about(splits[3], (KIDS, CH, CH), 1.0, 6.0, ((0, 2), (1, 8), (2, 8)), jnp.float32),
    }


def reference(anc_inverse, row_blocks, panel, diag_inverse):
    solved_list = []
    inverse_list = []
    for child_index in range(KIDS):
        offsets = jnp.arange(BS, dtype=jnp.int32)
        indices = (row_blocks[child_index][:, None] * BS + offsets[None, :]).reshape(-1).astype(jnp.int32)
        chosen = anc_inverse[indices[:, None], indices[None, :]]
        solved = -jnp.dot(chosen, panel[child_index], precision=lax.Precision.HIGHEST, preferred_element_type=jnp.float32)
        coupled = jnp.dot(panel[child_index].T, solved, precision=lax.Precision.HIGHEST, preferred_element_type=jnp.float32)
        inverse = diag_inverse[child_index] - 0.5 * (coupled + coupled.T)
        solved_list.append(solved)
        inverse_list.append(inverse)
    return jnp.stack(solved_list), jnp.stack(inverse_list)
```

```python
import jax
import jax.numpy as jnp
from jax import lax
from jax.experimental import pallas as pl
from jax.experimental.pallas import tpu as pltpu
from jax.sharding import PartitionSpec as P

AXES = ("gz", "row", "col")
VMEM_BYTES = 48 * 1024 * 1024


def send(array, place):
    pairs = []
    for gz in range(2):
        for row in range(8):
            for col in range(8):
                x, y, z, core = place(2 * (col // 4) + gz, row // 2, col % 4, row % 2)
                x, y, z = x % 4, y % 4, z % 4
                target = ((x % 2) * 8 + 2 * y + core) * 8 + 4 * (x // 2) + z
                pairs.append(((gz * 8 + row) * 8 + col, target))
    return lax.ppermute(array, AXES, pairs)


def shift(dx=0, dy=0, dz=0, core=0):
    return lambda x, y, z, k: (x + dx, y + dy, z + dz, k ^ core)


def transposed_place(x, y, z, core):
    return 2 * core + x % 2, z, y, x // 2


def spread_place(x, y, z, core):
    return 2 * ((x // 2) ^ (y // 2)) + x % 2, y, z ^ (2 * (y % 2) + core), core


def row_place(x, y, z, core):
    return x, y ^ (2 * (x // 2) + z // 2), z, core ^ (z % 2)


def halves(value):
    high = value.astype(jnp.bfloat16)
    return high, (value - high.astype(jnp.float32)).astype(jnp.bfloat16)


def product(left, right):
    def one(a, b):
        return jnp.dot(a, b, preferred_element_type=jnp.float32)

    return one(left[0], right[0]) + (one(left[0], right[1]) + one(left[1], right[0]))


def stage(refs, slots_ref, held, sems):
    copies = []
    for i, (ref, half) in enumerate(refs):
        target = held.at[slots_ref[i]]
        if half is not None:
            rows = ref.shape[0]
            target = target.at[half * rows : (half + 1) * rows]
        copies.append(pltpu.make_async_copy(ref, target, sems.at[i]))
    for copy in copies:
        copy.start()
    for copy in copies:
        copy.wait()


def row_product(blocks, strip, parts, slots, order, scale):
    count = len(blocks)
    pieces = len(strip)
    tile, width = blocks[0].shape[0], strip[0].shape[1]

    def body(slots_ref, order_ref, *refs):
        block_refs = refs[:count]
        strip_refs = refs[count : count + pieces]
        out_ref, held, sems = refs[count + pieces :]
        stage(list(zip(strip_refs, parts)), slots_ref, held, sems)
        for d in range(count):
            left = halves(block_refs[d][...])
            right = halves(held[order_ref[d]])
            term = scale * product(left, right)
            if d == 0:
                out_ref[...] = term
            else:
                out_ref[...] += term

    smem = pl.BlockSpec(memory_space=pltpu.SMEM)
    return pl.pallas_call(
        body,
        out_shape=jax.ShapeDtypeStruct((tile, width), jnp.float32),
        in_specs=[smem, smem]
        + [pl.BlockSpec(memory_space=pltpu.VMEM)] * count
        + [pl.BlockSpec(memory_space=pl.ANY)] * pieces,
        out_specs=pl.BlockSpec(memory_space=pltpu.VMEM),
        scratch_shapes=[
            pltpu.VMEM((count, tile, width), jnp.float32),
            pltpu.SemaphoreType.DMA((pieces,)),
        ],
        compiler_params=pltpu.CompilerParams(vmem_limit_bytes=VMEM_BYTES),
        cost_estimate=pl.CostEstimate(
            flops=6 * count * tile * tile * width,
            bytes_accessed=4 * (count + 2) * tile * (width + tile),
            transcendentals=0,
        ),
        name="row_product",
    )(slots, order, *blocks, *strip)


def block_product(base, lefts, strip, parts, slots, order):
    count = len(lefts)
    pieces = len(strip)
    width, tile = lefts[0].shape
    steps = width // tile

    def body(slots_ref, order_ref, base_ref, *refs):
        left_refs = refs[:count]
        strip_refs = refs[count : count + pieces]
        out_ref, held, high, low, sems = refs[count + pieces :]

        @pl.when(pl.program_id(0) == 0)
        def _():
            stage(list(zip(strip_refs, parts)), slots_ref, held, sems)
            for d in range(count):
                high[d], low[d] = halves(held[order_ref[d]])

        out_ref[...] = base_ref[...]
        for d in range(count):
            out_ref[...] += product(halves(left_refs[d][...]), (high[d], low[d]))

    smem = pl.BlockSpec(memory_space=pltpu.SMEM)
    return pl.pallas_call(
        body,
        grid=(steps,),
        out_shape=jax.ShapeDtypeStruct((width, width), jnp.float32),
        in_specs=[smem, smem, pl.BlockSpec((tile, width), lambda i: (i, 0))]
        + [pl.BlockSpec((tile, tile), lambda i: (i, 0))] * count
        + [pl.BlockSpec(memory_space=pl.ANY)] * pieces,
        out_specs=pl.BlockSpec((tile, width), lambda i: (i, 0)),
        scratch_shapes=[
            pltpu.VMEM((8, tile, width), jnp.float32),
            pltpu.VMEM((count, tile, width), jnp.bfloat16),
            pltpu.VMEM((count, tile, width), jnp.bfloat16),
            pltpu.SemaphoreType.DMA((pieces,)),
        ],
        compiler_params=pltpu.CompilerParams(vmem_limit_bytes=VMEM_BYTES),
        cost_estimate=pl.CostEstimate(
            flops=6 * count * tile * width * width,
            bytes_accessed=4 * (2 * width * width + (count + 8) * tile * width),
            transcendentals=0,
        ),
        name="block_product",
    )(slots, order, base, *lefts, *strip)


def row_gather(block):
    below, above = send(block, shift(dy=1)), send(block, shift(dy=-1))
    far = send(block, shift(dy=2))
    near = [block, below, above, far]
    return near + [send(piece, shift(core=1)) for piece in near]


def row_slots(y, core):
    places = [y, (y + 3) % 4, (y + 1) % 4, (y + 2) % 4]
    return jnp.stack([2 * p + core for p in places] + [2 * p + 1 - core for p in places])


def col_gather(block):
    partner = send(block, shift(dx=2))
    left, right = send(block, shift(dz=1)), send(block, shift(dz=-1))
    far = send(block, shift(dz=2))
    return [
        block,
        left,
        right,
        far,
        partner,
        send(partner, shift(dz=1)),
        send(partner, shift(dz=-1)),
        send(far, shift(dx=2)),
    ]


def col_places(half, z):
    around = [z, (z + 3) % 4, (z + 1) % 4, (z + 2) % 4]
    return [(half, p) for p in around] + [(1 - half, p) for p in around]


def chosen_piece(ancestor, row_blocks, gz, row, half, z, tile):
    x = 2 * half + gz
    lists = row_blocks.astype(jnp.int32)
    pair = lax.dynamic_slice_in_dim(lists, 2 * z, 2, axis=1)
    own = lax.dynamic_index_in_dim(lists, row, 1, keepdims=False)
    second = (pair[:, 1] // 16 == half).astype(jnp.int32)
    column = jnp.where(second == 1, pair[:, 1], pair[:, 0]) % 4
    holds = own // 16 == gz

    def contribution(step):
        target = (x + step) % 4
        child, slot = target % 2, target // 2
        portion = lax.dynamic_slice(
            ancestor, ((own[child] % 2) * tile, column[child] * tile), (tile, tile)
        )
        valid = jnp.logical_and(holds[child], second[child] == slot)
        return jnp.where(valid, portion, jnp.zeros_like(portion))

    total = contribution(0)
    for step in (1, 2, 3):
        total = total + send(contribution(step), shift(dx=step))
    return total


def per_device(anc_inverse, row_blocks, panel, diag_inverse):
    rows = panel[0]
    tile = rows.shape[0]
    gz, row, col = (lax.axis_index(name) for name in AXES)
    y, core, half, z = row // 2, row % 2, col // 4, col % 4

    slots = row_slots(y, core)
    places = col_places(half, z)
    chosen_order = jnp.stack([2 * p + h for h, p in places])
    panel_order = jnp.stack([row ^ (4 * h + p) for h, p in places])

    piece = chosen_piece(anc_inverse, row_blocks, gz, row, half, z, tile)
    other = send(piece, transposed_place)
    symmetric = 0.5 * (piece + other.T)

    strip = row_gather(rows)
    whole = [None] * 8
    moved = send(send(rows.T, spread_place), row_place)

    symmetric_row = col_gather(symmetric)
    chosen_row = col_gather(piece)
    half_coupled = row_product(symmetric_row, strip, whole, slots, chosen_order, 1.0)
    solved = row_product(chosen_row, strip, whole, slots, chosen_order, -1.0)

    coupled_strip = row_gather(half_coupled)
    panel_rows = col_gather(moved)
    child = block_product(
        diag_inverse[0], panel_rows, coupled_strip, whole, slots, panel_order
    )
    return solved[None], child[None]


def solution(mesh):
    return jax.shard_map(
        per_device,
        mesh=mesh,
        in_specs=(P(("gz", "row"), "col"), P(), P("gz", "row", "col"), P("gz", "row", "col")),
        out_specs=(P("gz", "row", "col"), P("gz", "row", "col")),
        check_vma=False,
    )
```

```python
import jax
import jax.numpy as jnp
from jax import lax
from jax.experimental import pallas as pl
from jax.experimental.pallas import tpu as pltpu
from jax.sharding import PartitionSpec as P

AXES = ("gz", "row", "col")
VMEM_BYTES = 62 * 1024 * 1024
ANY = pl.BlockSpec(memory_space=pl.ANY)
SMEM = pl.BlockSpec(memory_space=pltpu.SMEM)
WHOLE = pl.BlockSpec(memory_space=pltpu.VMEM)


def send(array, place):
    pairs = []
    for gz in range(2):
        for row in range(8):
            for col in range(8):
                x, y, z, core = place(2 * (col // 4) + gz, row // 2, col % 4, row % 2)
                x, y, z = x % 4, y % 4, z % 4
                target = ((x % 2) * 8 + 2 * y + core) * 8 + 4 * (x // 2) + z
                pairs.append(((gz * 8 + row) * 8 + col, target))
    return lax.ppermute(array, AXES, pairs)


def shift(dx=0, dy=0, dz=0, core=0):
    return lambda x, y, z, k: (x + dx, y + dy, z + dz, k ^ core)


def transposed_place(x, y, z, core):
    return x, y ^ z, z, core ^ (x // 2)


def spread_place(x, y, z, core):
    return 2 * ((x // 2) ^ (y // 2)) + x % 2, y, z ^ (2 * (y % 2) + core), core


def row_place(x, y, z, core):
    return x, y ^ (2 * (x // 2) + z // 2), z, core ^ (z % 2)


def together(*values):
    return lax.optimization_barrier(values)


def params():
    return pltpu.CompilerParams(vmem_limit_bytes=VMEM_BYTES)


def cost(flops, elements):
    return pl.CostEstimate(flops=1, bytes_accessed=1, transcendentals=0)


def halves(value):
    high = value.astype(jnp.bfloat16)
    return high, (value - high.astype(jnp.float32)).astype(jnp.bfloat16)


def product(left, right):
    def one(a, b):
        return jnp.dot(a, b, preferred_element_type=jnp.float32)

    return one(left[0], right[0]) + (one(left[0], right[1]) + one(left[1], right[0]))


def pick(ancestor, row_blocks, where, tile):
    def body(where_ref, lists_ref, ancestor_ref, own_ref, other_ref, held, sems):
        gz, row, half, z = (where_ref[i] for i in range(4))
        copies, holds = [], []
        for i, child in enumerate((gz, 1 - gz)):
            entry = lists_ref[child, row]
            first, second = lists_ref[child, 2 * z], lists_ref[child, 2 * z + 1]
            across = jnp.where(second // 16 == half, second, first)
            copies.append(
                pltpu.make_async_copy(
                    ancestor_ref.at[
                        pl.ds(pl.multiple_of((entry % 2) * tile, tile), tile),
                        pl.ds(pl.multiple_of((across % 4) * tile, tile), tile),
                    ],
                    held.at[i],
                    sems.at[i],
                )
            )
            holds.append(entry // 16 == gz)
        for copy in copies:
            copy.start()
        for i, out_ref in enumerate((own_ref, other_ref)):
            copies[i].wait()

            @pl.when(holds[i])
            def _():
                out_ref[...] = held[i]

            @pl.when(jnp.logical_not(holds[i]))
            def _():
                out_ref[...] = jnp.zeros((tile, tile), jnp.float32)

    return pl.pallas_call(
        body,
        out_shape=[jax.ShapeDtypeStruct((tile, tile), jnp.float32)] * 2,
        in_specs=[SMEM, SMEM, ANY],
        out_specs=[WHOLE] * 2,
        scratch_shapes=[
            pltpu.VMEM((2, tile, tile), jnp.float32),
            pltpu.SemaphoreType.DMA((2,)),
        ],
        compiler_params=params(),
        cost_estimate=cost(0, 4 * tile * tile),
        name="pick",
    )(where, row_blocks, ancestor)


def turned(block):
    tile, width = block.shape

    def body(block_ref, out_ref):
        out_ref[...] = block_ref[...].T

    return pl.pallas_call(
        body,
        grid=(width // tile,),
        out_shape=jax.ShapeDtypeStruct((width, tile), jnp.float32),
        in_specs=[pl.BlockSpec((tile, tile), lambda i: (0, i))],
        out_specs=pl.BlockSpec((tile, tile), lambda i: (i, 0)),
        compiler_params=params(),
        cost_estimate=cost(0, 2 * tile * width),
        name="turned",
    )(block)


def with_symmetric(piece, other):
    tile = piece.shape[0]

    def body(piece_ref, other_ref, out_ref):
        out_ref[:tile] = piece_ref[...]
        out_ref[tile:] = 0.5 * (piece_ref[...] + other_ref[...].T)

    return pl.pallas_call(
        body,
        out_shape=jax.ShapeDtypeStruct((2 * tile, tile), jnp.float32),
        in_specs=[WHOLE] * 2,
        out_specs=WHOLE,
        compiler_params=params(),
        cost_estimate=cost(0, 4 * piece.size),
        name="with_symmetric",
    )(piece, other)


def group_copies(groups, held, slots, sems):
    copies = []
    for i, group in enumerate(groups):
        start, out = 0, []
        for part, ref in enumerate(group):
            rows = ref.shape[0]
            target = held.at[slots[i], pl.ds(start, rows)]
            out.append(pltpu.make_async_copy(ref, target, sems.at[slots[i], part]))
            start += rows
        copies.append(out)
    return copies


def flat(groups):
    return [part for group in groups for part in group]


def grouped(refs, groups):
    out, start = [], 0
    for group in groups:
        out.append(refs[start : start + len(group)])
        start += len(group)
    return out


def row_product(blocks, start, block_slots, strip, strip_slots, scale):
    count, left_pieces, pieces = len(blocks), len(flat(blocks)), len(flat(strip))
    tile = blocks[0][0].shape[1]
    width = strip[0][0].shape[1]

    def body(block_slots_ref, strip_slots_ref, *refs):
        block_refs = []
        for group in grouped(refs[:left_pieces], blocks):
            if len(group) == 1:
                block_refs.append([group[0].at[pl.ds(start, tile)]])
            else:
                block_refs.append([group[start // tile]])
        strip_refs = grouped(refs[left_pieces : left_pieces + pieces], strip)
        out_ref, lefts, rights, left_sems, right_sems = refs[left_pieces + pieces :]
        left = group_copies(
            block_refs, lefts, [block_slots_ref[d] for d in range(count)], left_sems
        )
        right = group_copies(strip_refs, rights, list(range(count)), right_sems)
        for copy in flat(left) + flat(right):
            copy.start()
        for copy in flat(left):
            copy.wait()
        for i in range(count):
            for copy in right[i]:
                copy.wait()
            term = scale * product(halves(lefts[strip_slots_ref[i]]), halves(rights[i]))
            if i == 0:
                out_ref[...] = term
            else:
                out_ref[...] += term

    return pl.pallas_call(
        body,
        out_shape=jax.ShapeDtypeStruct((tile, width), jnp.float32),
        in_specs=[SMEM, SMEM] + [ANY] * (left_pieces + pieces),
        out_specs=WHOLE,
        scratch_shapes=[
            pltpu.VMEM((count, tile, tile), jnp.float32),
            pltpu.VMEM((count, tile, width), jnp.float32),
            pltpu.SemaphoreType.DMA((count, 1)),
            pltpu.SemaphoreType.DMA((count, 2)),
        ],
        compiler_params=params(),
        cost_estimate=cost(6 * count * tile * tile * width, (count + 2) * tile * (width + tile)),
        name="row_product",
    )(block_slots, strip_slots, *flat(blocks), *flat(strip))


def block_product(base, lefts, left_slots, left_used, strip, strip_slots, strip_used):
    count, left_pieces, strip_pieces = len(lefts), len(flat(lefts)), len(flat(strip))
    tile = lefts[0][0].shape[1]
    width = strip[0][0].shape[1]
    tiles = width // tile

    def body(left_slots_ref, left_used_ref, strip_slots_ref, strip_used_ref, base_ref, *refs):
        left_refs = grouped(refs[:left_pieces], lefts)
        refs = refs[left_pieces:]
        strip_refs = grouped(refs[:strip_pieces], strip)
        out_ref, total, left_held, right_held, base_sem, left_sems, right_sems, out_sems = refs[
            strip_pieces:
        ]
        first = pltpu.make_async_copy(base_ref, total, base_sem.at[0])
        left = group_copies(left_refs, left_held, list(range(count)), left_sems)
        right = group_copies(
            strip_refs,
            right_held,
            [strip_slots_ref[i] for i in range(len(strip))],
            right_sems,
        )
        for used_ref, groups in ((strip_used_ref, right), (left_used_ref, left)):
            for i, group in enumerate(groups):

                @pl.when(used_ref[i] == 1)
                def _():
                    for copy in group:
                        copy.start()

        first.start()
        for i, group in enumerate(right):

            @pl.when(strip_used_ref[i] == 1)
            def _():
                for copy in group:
                    copy.wait()

        first.wait()
        for d in range(count):

            @pl.when(left_used_ref[d] == 1)
            def _():
                for copy in left[d]:
                    copy.wait()
                right_parts = halves(right_held[left_slots_ref[d]])
                for t in range(tiles):
                    rows = pl.ds(t * tile, tile)
                    total[rows, :] += product(halves(left_held[d, rows, :]), right_parts)

        last = pltpu.make_async_copy(total, out_ref, out_sems.at[0])
        last.start()
        last.wait()

    return pl.pallas_call(
        body,
        out_shape=jax.ShapeDtypeStruct((width, width), jnp.float32),
        in_specs=[SMEM] * 4 + [ANY] * (1 + left_pieces + strip_pieces),
        out_specs=ANY,
        scratch_shapes=[
            pltpu.VMEM((width, width), jnp.float32),
            pltpu.VMEM((count, width, tile), jnp.float32),
            pltpu.VMEM((8, tile, width), jnp.float32),
            pltpu.SemaphoreType.DMA((1,)),
            pltpu.SemaphoreType.DMA((count, 2)),
            pltpu.SemaphoreType.DMA((8, 2)),
            pltpu.SemaphoreType.DMA((1,)),
        ],
        compiler_params=params(),
        cost_estimate=cost(
            6 * count * tile * width * width, 2 * width * width + 2 * count * tile * width
        ),
        name="block_product",
    )(left_slots, left_used, strip_slots, strip_used, base, *flat(lefts), *flat(strip))


def pass_on(below, above, **step):
    (axis, _), = step.items()
    middle = below.shape[0] // 2
    return [
        send(below[:middle], shift(**{axis: 1})),
        send(above[middle:], shift(**{axis: -1})),
    ]


def swap(group):
    return [send(part, shift(core=1)) for part in group]


def per_device(anc_inverse, row_blocks, panel, diag_inverse):
    rows = panel[0]
    tile = rows.shape[0]
    gz, row, col = (lax.axis_index(name) for name in AXES)
    y, core, half, z = row // 2, row % 2, col // 4, col % 4

    around = [z, (z + 3) % 4, (z + 1) % 4, (z + 2) % 4]
    places = [(half, p) for p in around] + [(1 - half, p) for p in around]
    chosen_slots = jnp.stack([row ^ (2 * p + h) for h, p in places])
    panel_slots = jnp.stack([row ^ (4 * h + p) for h, p in places])
    steps = [y, (y + 3) % 4, (y + 1) % 4, (y + 2) % 4]
    strip_slots = jnp.stack([2 * p + core for p in steps] + [2 * p + 1 - core for p in steps])

    below, above = send(rows, shift(dy=1)), send(rows, shift(dy=-1))
    own, other = pick(anc_inverse, row_blocks, jnp.stack([gz, row, half, z]), tile)
    mine = own + send(other, lambda x, y, z, k: (x ^ 1, y, z, k))
    own_list = lax.dynamic_index_in_dim(row_blocks, gz, 0, keepdims=False)
    stays = own_list[2 * z + (half ^ core)] // 16 == half
    piece = send(jnp.where(stays, mine, 0), lambda x, y, z, k: (x, y, z ^ y, k))
    piece += send(jnp.where(stays, 0, mine), lambda x, y, z, k: (x ^ 2, y, z ^ y, k))
    rows_turned = turned(rows)
    rows, piece, below, above, rows_turned = together(rows, piece, below, above, rows_turned)

    other = send(piece, transposed_place)
    spread = send(rows_turned, spread_place)
    swapped = [swap([part]) for part in (rows, below, above)]
    blocks = with_symmetric(piece, other)
    rows, below, above, blocks, spread, *swapped = together(
        rows, below, above, blocks, spread, *flat(swapped)
    )

    b_left, b_right = send(blocks, shift(dz=1)), send(blocks, shift(dz=-1))
    b_far, b_partner = send(blocks, shift(dz=2)), send(blocks, shift(dx=2))
    far = send(rows, shift(dy=2))
    b_left, b_right, b_far, b_partner, far, spread = together(
        b_left, b_right, b_far, b_partner, far, spread
    )
    b_partner_left, b_partner_right = send(b_partner, shift(dz=1)), send(b_partner, shift(dz=-1))
    b_partner_far = send(b_far, shift(dx=2))
    moved = send(spread, row_place)
    far_swapped = send(far, shift(core=1))
    b_partner_left, b_partner_right, b_partner_far, moved, far_swapped = together(
        b_partner_left, b_partner_right, b_partner_far, moved, far_swapped
    )
    all_blocks = [
        [block]
        for block in (
            blocks, b_left, b_right, b_far,
            b_partner, b_partner_left, b_partner_right, b_partner_far,
        )
    ]
    strip = [[part] for part in (rows, below, above, far, *swapped, far_swapped)]

    m_partner = send(moved, shift(dx=2))
    m_left, m_right = send(moved, shift(dz=1)), send(moved, shift(dz=-1))
    half_coupled = row_product(all_blocks, tile, chosen_slots, strip, strip_slots, 1.0)
    c_below, c_above = send(half_coupled, shift(dy=1)), send(half_coupled, shift(dy=-1))
    solved = row_product(all_blocks, 0, chosen_slots, strip, strip_slots, -1.0)
    half_coupled, solved, c_below, c_above, m_partner, m_left, m_right = together(
        half_coupled, solved, c_below, c_above, m_partner, m_left, m_right
    )
    m_far = send(m_left, shift(dz=1))
    m_partner_right = send(m_partner, shift(dz=-1))
    m_partner_left = send(m_left, shift(dx=2))
    c_far = pass_on(c_below, c_above, dy=1)
    half_coupled, m_far, m_partner_right, m_partner_left, *c_far = together(
        half_coupled, m_far, m_partner_right, m_partner_left, *c_far
    )
    m_partner_far = pass_on(m_partner_left, m_partner_right, dz=1)
    c_swapped = [swap([part]) for part in (half_coupled, c_below, c_above)]

    lefts = [
        [moved], [m_left], [m_right], [m_far], [m_partner], [m_partner_left], [m_partner_right],
    ]
    own_strip = [[half_coupled], [c_below], [c_above], c_far]
    late = jnp.concatenate([strip_slots[4:], panel_slots[7:]])

    def flags(slots, used):
        return (jnp.any(slots[:, None] == late[None, :], axis=1) == used).astype(jnp.int32)

    child = block_product(
        diag_inverse[0], lefts, panel_slots, flags(panel_slots, False),
        own_strip, strip_slots, flags(strip_slots, False),
    )
    *m_partner_far, s_own, s_below, s_above = together(*m_partner_far, *flat(c_swapped))
    child = block_product(
        child, lefts + [m_partner_far], panel_slots, flags(panel_slots, True),
        own_strip + [[s_own], [s_below], [s_above], swap(c_far)],
        strip_slots, flags(strip_slots, True),
    )
    return solved[None], child[None]


def solution(mesh):
    return jax.shard_map(
        per_device,
        mesh=mesh,
        in_specs=(P(("gz", "row"), "col"), P(), P("gz", "row", "col"), P("gz", "row", "col")),
        out_specs=(P("gz", "row", "col"), P("gz", "row", "col")),
        check_vma=False,
    )
```

```python
import jax
import jax.numpy as jnp
from jax import lax
from jax.experimental import pallas as pl
from jax.experimental.pallas import tpu as pltpu
from jax.sharding import PartitionSpec as P

AXES = ("gz", "row", "col")
VMEM_BYTES = 62 * 1024 * 1024
SMALL_VMEM_BYTES = 8 * 1024 * 1024
ANY = pl.BlockSpec(memory_space=pl.ANY)
SMEM = pl.BlockSpec(memory_space=pltpu.SMEM)
WHOLE = pl.BlockSpec(memory_space=pltpu.VMEM)


def send(array, place):
    pairs = []
    for gz in range(2):
        for row in range(8):
            for col in range(8):
                x, y, z, core = place(2 * (col // 4) + gz, row // 2, col % 4, row % 2)
                x, y, z = x % 4, y % 4, z % 4
                target = ((x % 2) * 8 + 2 * y + core) * 8 + 4 * (x // 2) + z
                pairs.append(((gz * 8 + row) * 8 + col, target))
    return lax.ppermute(array, AXES, pairs)


def shift(dx=0, dy=0, dz=0, core=0):
    return lambda x, y, z, k: (x + dx, y + dy, z + dz, k ^ core)


def spread_place(x, y, z, core):
    return 2 * ((x // 2) ^ (y // 2)) + x % 2, y, z ^ (2 * (y % 2) + core), core


def row_place(x, y, z, core):
    return x, y ^ (2 * (x // 2) + z // 2), z, core ^ (z % 2)


def column_places(half, z):
    around = [z, (z + 3) & 3, (z + 1) & 3, (z + 2) & 3]
    return [(half, p) for p in around] + [(1 - half, p) for p in around]


def chosen_slots(lists, child, half, z):
    return [2 * p + held_second(lists, child, h, p) for h, p in column_places(half, z)]


def turned_slots(lists, child, row, half, z):
    high = lists[child, row] // 16
    return [2 * (p ^ (row >> 1)) + (h ^ high) for h, p in column_places(half, z)]


def held_second(lists, child, half, z):
    return (lists[child, 2 * z + 1] // 16 == half).astype(jnp.int32)


def panel_slots(row, half, z):
    return [row ^ (4 * h + p) for h, p in column_places(half, z)]


def strip_slots(row):
    y, core = row >> 1, row & 1
    steps = [y, (y + 3) & 3, (y + 1) & 3, (y + 2) & 3]
    return [2 * p + core for p in steps] + [2 * p + 1 - core for p in steps]


def together(*values):
    return lax.optimization_barrier(values)


def params(limit=VMEM_BYTES):
    return pltpu.CompilerParams(vmem_limit_bytes=limit)


def cost(flops, elements):
    return pl.CostEstimate(flops=1, bytes_accessed=1, transcendentals=0)


def halves(value):
    high = value.astype(jnp.bfloat16)
    return high, (value - high.astype(jnp.float32)).astype(jnp.bfloat16)


def product(left, right):
    def one(a, b):
        return jnp.dot(a, b, preferred_element_type=jnp.float32)

    return one(left[0], right[0]) + (one(left[0], right[1]) + one(left[1], right[0]))


def pick(ancestor, row_blocks, where, tile):
    def body(where_ref, lists_ref, ancestor_ref, own_ref, other_ref, held, sems):
        gz, row, half, z = (where_ref[i] for i in range(4))
        copies, holds = [], []
        for i, child in enumerate((gz, 1 - gz)):
            entry = lists_ref[child, row]
            first, second = lists_ref[child, 2 * z], lists_ref[child, 2 * z + 1]
            across = jnp.where(second // 16 == half, second, first)
            copies.append(
                pltpu.make_async_copy(
                    ancestor_ref.at[
                        pl.ds(pl.multiple_of((entry % 2) * tile, tile), tile),
                        pl.ds(pl.multiple_of((across % 4) * tile, tile), tile),
                    ],
                    held.at[i],
                    sems.at[i],
                )
            )
            holds.append(entry // 16 == gz)
        for copy in copies:
            copy.start()
        for i, out_ref in enumerate((own_ref, other_ref)):
            copies[i].wait()

            @pl.when(holds[i])
            def _():
                out_ref[...] = held[i]

            @pl.when(jnp.logical_not(holds[i]))
            def _():
                out_ref[...] = jnp.zeros((tile, tile), jnp.float32)

    return pl.pallas_call(
        body,
        out_shape=[jax.ShapeDtypeStruct((tile, tile), jnp.float32)] * 2,
        in_specs=[SMEM, SMEM, ANY],
        out_specs=[WHOLE] * 2,
        scratch_shapes=[
            pltpu.VMEM((2, tile, tile), jnp.float32),
            pltpu.SemaphoreType.DMA((2,)),
        ],
        compiler_params=params(),
        cost_estimate=cost(0, 4 * tile * tile),
        name="pick",
    )(where, row_blocks, ancestor)


def joined(first, second):
    def body(first_ref, second_ref, out_ref):
        out_ref[...] = first_ref[...] + second_ref[...]

    return pl.pallas_call(
        body,
        out_shape=jax.ShapeDtypeStruct(first.shape, jnp.float32),
        in_specs=[WHOLE] * 2,
        out_specs=WHOLE,
        compiler_params=params(SMALL_VMEM_BYTES),
        cost_estimate=cost(0, 3 * first.size),
        name="joined",
    )(first, second)


def sort_piece(piece, where, row_blocks):
    def body(where_ref, lists_ref, piece_ref, same_ref, other_ref):
        gz, row, half, z = (where_ref[i] for i in range(4))
        core = row & 1
        is_same = held_second(lists_ref, gz, half ^ core, z ^ (row >> 1)) == core

        @pl.when(is_same)
        def _():
            same_ref[...] = piece_ref[...]
            other_ref[...] = jnp.zeros(piece.shape, jnp.float32)

        @pl.when(jnp.logical_not(is_same))
        def _():
            same_ref[...] = jnp.zeros(piece.shape, jnp.float32)
            other_ref[...] = piece_ref[...]

    return pl.pallas_call(
        body,
        out_shape=[jax.ShapeDtypeStruct(piece.shape, jnp.float32)] * 2,
        in_specs=[SMEM, SMEM, WHOLE],
        out_specs=[WHOLE] * 2,
        compiler_params=params(SMALL_VMEM_BYTES),
        cost_estimate=cost(0, 3 * piece.size),
        name="sort_piece",
    )(where, row_blocks, piece)


def turned(block):
    tile, width = block.shape

    def body(block_ref, out_ref):
        out_ref[...] = block_ref[...].T

    return pl.pallas_call(
        body,
        grid=(width // tile,),
        out_shape=jax.ShapeDtypeStruct((width, tile), jnp.float32),
        in_specs=[pl.BlockSpec((tile, tile), lambda i: (0, i))],
        out_specs=pl.BlockSpec((tile, tile), lambda i: (i, 0)),
        compiler_params=params(SMALL_VMEM_BYTES),
        cost_estimate=cost(0, 2 * tile * width),
        name="turned",
    )(block)


def stacked(mine, first, second):
    tile = mine.shape[0]

    def body(mine_ref, first_ref, second_ref, out_ref):
        out_ref[:tile] = mine_ref[...]
        out_ref[tile:] = (first_ref[...] + second_ref[...]).T

    return pl.pallas_call(
        body,
        out_shape=jax.ShapeDtypeStruct((2 * tile, tile), jnp.float32),
        in_specs=[WHOLE] * 3,
        out_specs=WHOLE,
        compiler_params=params(SMALL_VMEM_BYTES),
        cost_estimate=cost(0, 5 * mine.size),
        name="stacked",
    )(mine, first, second)


def group_copies(groups, held, slots, sems):
    copies = []
    for i, group in enumerate(groups):
        start, out = 0, []
        for part, ref in enumerate(group):
            rows = ref.shape[0]
            target = held.at[slots[i], pl.ds(start, rows)]
            out.append(pltpu.make_async_copy(ref, target, sems.at[slots[i], part]))
            start += rows
        copies.append(out)
    return copies


def flat(groups):
    return [part for group in groups for part in group]


def grouped(refs, groups):
    out, start = [], 0
    for group in groups:
        out.append(refs[start : start + len(group)])
        start += len(group)
    return out


def row_product(blocks, strip, where, row_blocks, symmetric):
    count = len(blocks)
    tile, width = blocks[0].shape[1], strip[0].shape[1]
    parts = 2 if symmetric else 1

    def body(where_ref, lists_ref, *refs):
        block_refs, strip_refs = refs[:count], refs[count : 2 * count]
        out_ref, lefts, rights, left_sems, right_sems = refs[2 * count :]
        gz, row, half, z = (where_ref[i] for i in range(4))
        slots = [chosen_slots(lists_ref, gz, half, z), turned_slots(lists_ref, gz, row, half, z)]
        left = [
            pltpu.make_async_copy(
                block_refs[d].at[pl.ds(part * tile, tile)],
                lefts.at[part, slots[part][d]],
                left_sems.at[part, d],
            )
            for part in range(parts)
            for d in range(count)
        ]
        right = [
            pltpu.make_async_copy(strip_refs[i], rights.at[i], right_sems.at[i])
            for i in range(count)
        ]
        for copy in left + right[:2]:
            copy.start()
        for copy in left:
            copy.wait()
        for i, slot in enumerate(strip_slots(row)):
            right[i].wait()
            if i + 2 < count:
                right[i + 2].start()
            block = 0.5 * (lefts[0, slot] + lefts[1, slot]) if symmetric else -lefts[0, slot]
            term = product(halves(block), halves(rights[i]))
            if i == 0:
                out_ref[...] = term
            else:
                out_ref[...] += term

    return pl.pallas_call(
        body,
        out_shape=jax.ShapeDtypeStruct((tile, width), jnp.float32),
        in_specs=[SMEM, SMEM] + [ANY] * (2 * count),
        out_specs=WHOLE,
        scratch_shapes=[
            pltpu.VMEM((parts, count, tile, tile), jnp.float32),
            pltpu.VMEM((count, tile, width), jnp.float32),
            pltpu.SemaphoreType.DMA((parts, count)),
            pltpu.SemaphoreType.DMA((count,)),
        ],
        compiler_params=params(),
        cost_estimate=cost(6 * count * tile * tile * width, (count + 2) * tile * (width + tile)),
        name="row_product",
    )(where, row_blocks, *blocks, *strip)


def block_product(base, lefts, strip, where, first_late, late):
    count, rights = len(lefts), len(strip)
    left_pieces, strip_pieces = len(flat(lefts)), len(flat(strip))
    tile = lefts[0][0].shape[1]
    width = strip[0][0].shape[1]
    ahead = 3

    def body(where_ref, base_ref, *refs):
        left_refs = grouped(refs[:left_pieces], lefts)
        refs = refs[left_pieces:]
        strip_refs = grouped(refs[:strip_pieces], strip)
        (
            out_ref, total, base_held, left_held, right_held,
            base_sem, left_sems, right_sems, out_sems,
        ) = refs[strip_pieces:]
        row, half, z = (where_ref[i] for i in (1, 2, 3))
        left_slots, right_slots = panel_slots(row, half, z), strip_slots(row)
        late_slots = right_slots[first_late:] + left_slots[7:]

        def used(slot):
            found = slot == late_slots[0]
            for other in late_slots[1:]:
                found = jnp.logical_or(found, slot == other)
            return found if late else jnp.logical_not(found)

        base_copy = pltpu.make_async_copy(base_ref, base_held, base_sem.at[0])
        left = group_copies(left_refs, left_held, list(range(count)), left_sems)
        right = group_copies(strip_refs, right_held, right_slots, right_sems)
        for i in range(rights):

            @pl.when(used(right_slots[i]))
            def _():
                for copy in right[i]:
                    copy.start()

        def fetch(d):
            @pl.when(used(left_slots[d]))
            def _():
                for copy in left[d]:
                    copy.start()

        for d in range(min(ahead, count)):
            fetch(d)
        base_copy.start()
        total[...] = jnp.zeros_like(total)
        for i in range(rights):

            @pl.when(used(right_slots[i]))
            def _():
                for copy in right[i]:
                    copy.wait()

        for d in range(count):
            if d + ahead < count:
                fetch(d + ahead)

            @pl.when(used(left_slots[d]))
            def _():
                for copy in left[d]:
                    copy.wait()
                right_parts = halves(right_held[left_slots[d]])
                for t in range(0, width, tile):
                    rows = pl.ds(t, tile)
                    total[rows, :] += product(halves(left_held[d, rows, :]), right_parts)

        base_copy.wait()
        results = []
        for t in range(0, width, tile):
            rows = pl.ds(t, tile)
            total[rows, :] += base_held[rows, :]
            results.append(
                pltpu.make_async_copy(total.at[rows], out_ref.at[rows], out_sems.at[t // tile])
            )
            results[-1].start()
        for copy in results:
            copy.wait()

    return pl.pallas_call(
        body,
        out_shape=jax.ShapeDtypeStruct((width, width), jnp.float32),
        in_specs=[SMEM] + [ANY] * (1 + left_pieces + strip_pieces),
        out_specs=ANY,
        scratch_shapes=[
            pltpu.VMEM((width, width), jnp.float32),
            pltpu.VMEM((width, width), jnp.float32),
            pltpu.VMEM((count, width, tile), jnp.float32),
            pltpu.VMEM((8, tile, width), jnp.float32),
            pltpu.SemaphoreType.DMA((1,)),
            pltpu.SemaphoreType.DMA((count, 2)),
            pltpu.SemaphoreType.DMA((8, 2)),
            pltpu.SemaphoreType.DMA((width // tile,)),
        ],
        compiler_params=params(),
        cost_estimate=cost(
            6 * count * tile * width * width, 2 * width * width + 2 * count * tile * width
        ),
        name="block_product",
    )(where, base, *flat(lefts), *flat(strip))


def top(array):
    return array[: array.shape[0] // 2]


def bottom(array):
    return array[array.shape[0] // 2 :]


def per_device(anc_inverse, row_blocks, panel, diag_inverse):
    rows = panel[0]
    tile = rows.shape[0]
    gz, row, col = (lax.axis_index(name) for name in AXES)
    where = jnp.stack([gz, row, col // 4, col % 4])
    other_core, across, back, forth = shift(core=1), shift(dx=2), shift(dz=-1), shift(dz=1)

    below, above = send(rows, shift(dy=1)), send(rows, shift(dy=-1))
    own, other = pick(anc_inverse, row_blocks, where, tile)
    mine = joined(own, send(other, lambda x, y, z, k: (x ^ 1, y, z, k)))
    piece = send(mine, lambda x, y, z, k: (x ^ (2 * k), y, z ^ y, k))
    same, other = sort_piece(piece, where, row_blocks)
    rows_turned = turned(rows)
    s_own = send(rows, other_core)
    rows, mine, same, other, below, above, s_own, rows_turned = together(
        rows, mine, same, other, below, above, s_own, rows_turned
    )

    same = send(same, lambda x, y, z, k: (x, y ^ z, z, k))
    other = send(other, lambda x, y, z, k: (x, y ^ z, z, k ^ 1))
    spread = send(rows_turned, spread_place)
    s_below, s_above = send(below, other_core), send(above, other_core)
    blocks = stacked(mine, same, other)
    rows, blocks, s_below, s_above = together(rows, blocks, s_below, s_above)

    b_left, b_right = send(blocks, forth), send(blocks, back)
    b_far, b_partner = send(blocks, shift(dz=2)), send(blocks, across)
    far = send(rows, shift(dy=2))
    spread, _ = together(spread, b_left)
    moved = send(spread, row_place)
    b_left, b_right, b_far, b_partner, far = together(b_left, b_right, b_far, b_partner, far)
    b_partner_left, b_partner_right = send(b_partner, forth), send(b_partner, back)
    b_partner_far = send(b_far, across)
    s_far = send(far, other_core)
    moved, b_partner_left, b_partner_right, b_partner_far, s_far = together(
        moved, b_partner_left, b_partner_right, b_partner_far, s_far
    )
    all_blocks = [
        blocks, b_left, b_right, b_far,
        b_partner, b_partner_left, b_partner_right, b_partner_far,
    ]
    strip = [rows, below, above, far, s_own, s_below, s_above, s_far]

    m_partner = send(moved, across)
    m_left, m_right = send(moved, forth), send(moved, back)
    half_coupled = row_product(all_blocks, strip, where, row_blocks, True)
    c_below, c_above = send(half_coupled, shift(dy=1)), send(half_coupled, shift(dy=-1))
    where_late, _ = together(where, half_coupled)
    solved = row_product(all_blocks, strip, where_late, row_blocks, False)
    m_partner, m_left, m_right, _ = together(m_partner, m_left, m_right, half_coupled)
    m_far = send(m_left, forth)
    m_partner_right = send(m_partner, back)
    m_partner_left = send(m_left, across)
    solved, c_below, c_above = together(solved, c_below, c_above)
    c_top, c_bottom, m_top, m_bottom, m_far, half_coupled = together(
        top(c_below), bottom(c_above), top(m_partner_left), bottom(m_partner_right),
        m_far, half_coupled,
    )
    c_far = [send(c_top, shift(dy=1)), send(c_bottom, shift(dy=-1))]
    m_partner_far = [send(m_top, forth), send(m_bottom, back)]
    t_own = send(half_coupled, other_core)
    t_below, t_above, *c_far = together(c_below, c_above, *c_far)
    t_far = [send(part, other_core) for part in c_far]
    t_below, t_above = send(t_below, other_core), send(t_above, other_core)

    lefts = [
        [moved], [m_left], [m_right], [m_far], [m_partner], [m_partner_left], [m_partner_right],
    ]
    own_strip = [[half_coupled], [c_below], [c_above]]
    where_late, *c_far = together(where, *c_far)
    child = block_product(diag_inverse[0], lefts, own_strip, where_late, 3, False)
    child = block_product(
        child,
        lefts + [m_partner_far],
        own_strip + [c_far, [t_own], [t_below], [t_above], t_far],
        where,
        3,
        True,
    )
    return solved[None], child[None]


def solution(mesh):
    return jax.shard_map(
        per_device,
        mesh=mesh,
        in_specs=(P(("gz", "row"), "col"), P(), P("gz", "row", "col"), P("gz", "row", "col")),
        out_specs=(P("gz", "row", "col"), P("gz", "row", "col")),
        check_vma=False,
    )
```

```python
import jax
import jax.numpy as jnp
from jax import lax
from jax.experimental import pallas as pl
from jax.experimental.pallas import tpu as pltpu
from jax.sharding import PartitionSpec as P

AXES = ("gz", "row", "col")
VMEM_BYTES = 62 * 1024 * 1024
SMALL_VMEM_BYTES = 8 * 1024 * 1024
ANY = pl.BlockSpec(memory_space=pl.ANY)
SMEM = pl.BlockSpec(memory_space=pltpu.SMEM)
WHOLE = pl.BlockSpec(memory_space=pltpu.VMEM)


def send(array, place):
    pairs = []
    for gz in range(2):
        for row in range(8):
            for col in range(8):
                x, y, z, core = place(2 * (col // 4) + gz, row // 2, col % 4, row % 2)
                x, y, z = x % 4, y % 4, z % 4
                target = ((x % 2) * 8 + 2 * y + core) * 8 + 4 * (x // 2) + z
                pairs.append(((gz * 8 + row) * 8 + col, target))
    return lax.ppermute(array, AXES, pairs)


def shift(dx=0, dy=0, dz=0, core=0):
    return lambda x, y, z, k: (x + dx, y + dy, z + dz, k ^ core)


def spread_place(x, y, z, core):
    return 2 * ((x // 2) ^ (y // 2)) + x % 2, y, z ^ (2 * (y % 2) + core), core


def row_place(x, y, z, core):
    return x, y ^ (2 * (x // 2) + z // 2), z, core ^ (z % 2)


def column_places(half, z):
    around = [z, (z + 3) & 3, (z + 1) & 3, (z + 2) & 3]
    return [(half, p) for p in around] + [(1 - half, p) for p in around]


def chosen_slots(lists, child, half, z):
    return [2 * p + held_second(lists, child, h, p) for h, p in column_places(half, z)]


def turned_slots(lists, child, row, half, z):
    high = lists[child, row] // 16
    return [2 * (p ^ (row >> 1)) + (h ^ high) for h, p in column_places(half, z)]


def held_second(lists, child, half, z):
    return (lists[child, 2 * z + 1] // 16 == half).astype(jnp.int32)


def panel_slots(row, half, z):
    return [row ^ (4 * h + p) for h, p in column_places(half, z)]


def strip_slots(row):
    y, core = row >> 1, row & 1
    steps = [y, (y + 3) & 3, (y + 1) & 3, (y + 2) & 3]
    return [2 * p + core for p in steps] + [2 * p + 1 - core for p in steps]


def together(*values):
    return lax.optimization_barrier(values)


def params(limit=VMEM_BYTES):
    return pltpu.CompilerParams(vmem_limit_bytes=limit)


def cost(flops, elements):
    return pl.CostEstimate(flops=1, bytes_accessed=1, transcendentals=0)


def halves(value):
    high = value.astype(jnp.bfloat16)
    return high, (value - high.astype(jnp.float32)).astype(jnp.bfloat16)


def product(left, right):
    def one(a, b):
        return jnp.dot(a, b, preferred_element_type=jnp.float32)

    return one(left[0], right[0]) + (one(left[0], right[1]) + one(left[1], right[0]))


def pick(ancestor, row_blocks, where, tile):
    def body(where_ref, lists_ref, ancestor_ref, own_ref, other_ref, held, sems):
        gz, row, half, z = (where_ref[i] for i in range(4))
        copies, holds = [], []
        for i, child in enumerate((gz, 1 - gz)):
            entry = lists_ref[child, row]
            first, second = lists_ref[child, 2 * z], lists_ref[child, 2 * z + 1]
            across = jnp.where(second // 16 == half, second, first)
            copies.append(
                pltpu.make_async_copy(
                    ancestor_ref.at[
                        pl.ds(pl.multiple_of((entry % 2) * tile, tile), tile),
                        pl.ds(pl.multiple_of((across % 4) * tile, tile), tile),
                    ],
                    held.at[i],
                    sems.at[i],
                )
            )
            holds.append(entry // 16 == gz)
        for copy in copies:
            copy.start()
        for i, out_ref in enumerate((own_ref, other_ref)):
            copies[i].wait()

            @pl.when(holds[i])
            def _():
                out_ref[...] = held[i]

            @pl.when(jnp.logical_not(holds[i]))
            def _():
                out_ref[...] = jnp.zeros((tile, tile), jnp.float32)

    return pl.pallas_call(
        body,
        out_shape=[jax.ShapeDtypeStruct((tile, tile), jnp.float32)] * 2,
        in_specs=[SMEM, SMEM, ANY],
        out_specs=[WHOLE] * 2,
        scratch_shapes=[
            pltpu.VMEM((2, tile, tile), jnp.float32),
            pltpu.SemaphoreType.DMA((2,)),
        ],
        compiler_params=params(),
        cost_estimate=cost(0, 4 * tile * tile),
        name="pick",
    )(where, row_blocks, ancestor)


def joined(first, second):
    def body(first_ref, second_ref, out_ref):
        out_ref[...] = first_ref[...] + second_ref[...]

    return pl.pallas_call(
        body,
        out_shape=jax.ShapeDtypeStruct(first.shape, jnp.float32),
        in_specs=[WHOLE] * 2,
        out_specs=WHOLE,
        compiler_params=params(SMALL_VMEM_BYTES),
        cost_estimate=cost(0, 3 * first.size),
        name="joined",
    )(first, second)


def sort_piece(piece, where, row_blocks):
    def body(where_ref, lists_ref, piece_ref, same_ref, other_ref):
        gz, row, half, z = (where_ref[i] for i in range(4))
        core = row & 1
        is_same = held_second(lists_ref, gz, half ^ core, z ^ (row >> 1)) == core

        @pl.when(is_same)
        def _():
            same_ref[...] = piece_ref[...]
            other_ref[...] = jnp.zeros(piece.shape, jnp.float32)

        @pl.when(jnp.logical_not(is_same))
        def _():
            same_ref[...] = jnp.zeros(piece.shape, jnp.float32)
            other_ref[...] = piece_ref[...]

    return pl.pallas_call(
        body,
        out_shape=[jax.ShapeDtypeStruct(piece.shape, jnp.float32)] * 2,
        in_specs=[SMEM, SMEM, WHOLE],
        out_specs=[WHOLE] * 2,
        compiler_params=params(SMALL_VMEM_BYTES),
        cost_estimate=cost(0, 3 * piece.size),
        name="sort_piece",
    )(where, row_blocks, piece)


def turned(block):
    tile, width = block.shape

    def body(block_ref, out_ref):
        out_ref[...] = block_ref[...].T

    return pl.pallas_call(
        body,
        grid=(width // tile,),
        out_shape=jax.ShapeDtypeStruct((width, tile), jnp.float32),
        in_specs=[pl.BlockSpec((tile, tile), lambda i: (0, i))],
        out_specs=pl.BlockSpec((tile, tile), lambda i: (i, 0)),
        compiler_params=params(SMALL_VMEM_BYTES),
        cost_estimate=cost(0, 2 * tile * width),
        name="turned",
    )(block)


def stacked(mine, first, second):
    tile = mine.shape[0]

    def body(mine_ref, first_ref, second_ref, out_ref):
        out_ref[:tile] = mine_ref[...]
        out_ref[tile:] = (first_ref[...] + second_ref[...]).T

    return pl.pallas_call(
        body,
        out_shape=jax.ShapeDtypeStruct((2 * tile, tile), jnp.float32),
        in_specs=[WHOLE] * 3,
        out_specs=WHOLE,
        compiler_params=params(SMALL_VMEM_BYTES),
        cost_estimate=cost(0, 5 * mine.size),
        name="stacked",
    )(mine, first, second)


def group_copies(groups, held, slots, sems):
    copies = []
    for i, group in enumerate(groups):
        start, out = 0, []
        for part, ref in enumerate(group):
            rows = ref.shape[0]
            target = held.at[slots[i], pl.ds(start, rows)]
            out.append(pltpu.make_async_copy(ref, target, sems.at[slots[i], part]))
            start += rows
        copies.append(out)
    return copies


def flat(groups):
    return [part for group in groups for part in group]


def grouped(refs, groups):
    out, start = [], 0
    for group in groups:
        out.append(refs[start : start + len(group)])
        start += len(group)
    return out


def row_product(blocks, strip, where, row_blocks, symmetric):
    count = len(blocks)
    tile, width = blocks[0].shape[1], strip[0].shape[1]
    parts = 2 if symmetric else 1

    def body(where_ref, lists_ref, *refs):
        block_refs, strip_refs = refs[:count], refs[count : 2 * count]
        out_ref, lefts, rights, left_sems, right_sems = refs[2 * count :]
        gz, row, half, z = (where_ref[i] for i in range(4))
        slots = [chosen_slots(lists_ref, gz, half, z), turned_slots(lists_ref, gz, row, half, z)]
        left = [
            pltpu.make_async_copy(
                block_refs[d].at[pl.ds(part * tile, tile)],
                lefts.at[part, slots[part][d]],
                left_sems.at[part, d],
            )
            for part in range(parts)
            for d in range(count)
        ]
        right = [
            pltpu.make_async_copy(strip_refs[i], rights.at[i], right_sems.at[i])
            for i in range(count)
        ]
        for copy in left + right[:2]:
            copy.start()
        for copy in left:
            copy.wait()
        for i, slot in enumerate(strip_slots(row)):
            right[i].wait()
            if i + 2 < count:
                right[i + 2].start()
            block = 0.5 * (lefts[0, slot] + lefts[1, slot]) if symmetric else -lefts[0, slot]
            term = product(halves(block), halves(rights[i]))
            if i == 0:
                out_ref[...] = term
            else:
                out_ref[...] += term

    return pl.pallas_call(
        body,
        out_shape=jax.ShapeDtypeStruct((tile, width), jnp.float32),
        in_specs=[SMEM, SMEM] + [ANY] * (2 * count),
        out_specs=WHOLE,
        scratch_shapes=[
            pltpu.VMEM((parts, count, tile, tile), jnp.float32),
            pltpu.VMEM((count, tile, width), jnp.float32),
            pltpu.SemaphoreType.DMA((parts, count)),
            pltpu.SemaphoreType.DMA((count,)),
        ],
        compiler_params=params(),
        cost_estimate=cost(6 * count * tile * tile * width, (count + 2) * tile * (width + tile)),
        name="row_product",
    )(where, row_blocks, *blocks, *strip)


def block_product(base, lefts, strip, where, first_late, late):
    count, rights = len(lefts), len(strip)
    left_pieces, strip_pieces = len(flat(lefts)), len(flat(strip))
    tile = lefts[0][0].shape[1]
    width = strip[0][0].shape[1]
    ahead = 3

    def body(where_ref, base_ref, *refs):
        left_refs = grouped(refs[:left_pieces], lefts)
        refs = refs[left_pieces:]
        strip_refs = grouped(refs[:strip_pieces], strip)
        (
            out_ref, total, base_held, left_held, right_held,
            base_sem, left_sems, right_sems, out_sems,
        ) = refs[strip_pieces:]
        row, half, z = (where_ref[i] for i in (1, 2, 3))
        left_slots, right_slots = panel_slots(row, half, z), strip_slots(row)
        late_slots = right_slots[first_late:] + left_slots[7:]

        def used(slot):
            found = slot == late_slots[0]
            for other in late_slots[1:]:
                found = jnp.logical_or(found, slot == other)
            return found if late else jnp.logical_not(found)

        base_copy = pltpu.make_async_copy(base_ref, base_held, base_sem.at[0])
        left = group_copies(left_refs, left_held, list(range(count)), left_sems)

        def right_copies(d):
            return group_copies(strip_refs, right_held, [d] * rights, right_sems)

        def matching(d, act):
            for i, copies in enumerate(right_copies(d)):

                @pl.when(jnp.logical_and(used(left_slots[d]), right_slots[i] == left_slots[d]))
                def _():
                    for copy in copies:
                        act(copy)

        def fetch(d):
            matching(d, lambda copy: copy.start())

            @pl.when(used(left_slots[d]))
            def _():
                for copy in left[d]:
                    copy.start()

        for d in range(min(ahead, count)):
            fetch(d)
        total[...] = jnp.zeros_like(total)
        for d in range(count):
            if d + ahead < count:
                fetch(d + ahead)
            if d + ahead == count:
                base_copy.start()
            matching(d, lambda copy: copy.wait())

            @pl.when(used(left_slots[d]))
            def _():
                for copy in left[d]:
                    copy.wait()
                right_parts = halves(right_held[d])
                for t in range(0, width, tile):
                    rows = pl.ds(t, tile)
                    total[rows, :] += product(halves(left_held[d, rows, :]), right_parts)

        base_copy.wait()
        results = []
        for t in range(0, width, tile):
            rows = pl.ds(t, tile)
            total[rows, :] += base_held[rows, :]
            results.append(
                pltpu.make_async_copy(total.at[rows], out_ref.at[rows], out_sems.at[t // tile])
            )
            results[-1].start()
        for copy in results:
            copy.wait()

    return pl.pallas_call(
        body,
        out_shape=jax.ShapeDtypeStruct((width, width), jnp.float32),
        in_specs=[SMEM] + [ANY] * (1 + left_pieces + strip_pieces),
        out_specs=ANY,
        scratch_shapes=[
            pltpu.VMEM((width, width), jnp.float32),
            pltpu.VMEM((width, width), jnp.float32),
            pltpu.VMEM((count, width, tile), jnp.float32),
            pltpu.VMEM((8, tile, width), jnp.float32),
            pltpu.SemaphoreType.DMA((1,)),
            pltpu.SemaphoreType.DMA((count, 2)),
            pltpu.SemaphoreType.DMA((8, 2)),
            pltpu.SemaphoreType.DMA((width // tile,)),
        ],
        compiler_params=params(),
        cost_estimate=cost(
            6 * count * tile * width * width, 2 * width * width + 2 * count * tile * width
        ),
        name="block_product",
    )(where, base, *flat(lefts), *flat(strip))


def top(array):
    return array[: array.shape[0] // 2]


def bottom(array):
    return array[array.shape[0] // 2 :]


def per_device(anc_inverse, row_blocks, panel, diag_inverse):
    rows = panel[0]
    tile = rows.shape[0]
    gz, row, col = (lax.axis_index(name) for name in AXES)
    where = jnp.stack([gz, row, col // 4, col % 4])
    other_core, across, back, forth = shift(core=1), shift(dx=2), shift(dz=-1), shift(dz=1)

    below, above = send(rows, shift(dy=1)), send(rows, shift(dy=-1))
    own, other = pick(anc_inverse, row_blocks, where, tile)
    mine = joined(own, send(other, lambda x, y, z, k: (x ^ 1, y, z, k)))
    piece = send(mine, lambda x, y, z, k: (x ^ (2 * k), y, z ^ y, k))
    same, other = sort_piece(piece, where, row_blocks)
    rows_turned = turned(rows)
    s_own = send(rows, other_core)
    rows, mine, same, other, below, above, s_own, rows_turned = together(
        rows, mine, same, other, below, above, s_own, rows_turned
    )

    same = send(same, lambda x, y, z, k: (x, y ^ z, z, k))
    other = send(other, lambda x, y, z, k: (x, y ^ z, z, k ^ 1))
    spread = send(rows_turned, spread_place)
    s_below, s_above = send(below, other_core), send(above, other_core)
    blocks = stacked(mine, same, other)
    rows, blocks, s_below, s_above = together(rows, blocks, s_below, s_above)

    b_left, b_right = send(blocks, forth), send(blocks, back)
    b_far, b_partner = send(blocks, shift(dz=2)), send(blocks, across)
    far = send(rows, shift(dy=2))
    spread, _ = together(spread, b_left)
    moved = send(spread, row_place)
    b_left, b_right, b_far, b_partner, far = together(b_left, b_right, b_far, b_partner, far)
    b_partner_left, b_partner_right = send(b_partner, forth), send(b_partner, back)
    b_partner_far = send(b_far, across)
    s_far = send(far, other_core)
    moved, b_partner_left, b_partner_right, b_partner_far, s_far = together(
        moved, b_partner_left, b_partner_right, b_partner_far, s_far
    )
    all_blocks = [
        blocks, b_left, b_right, b_far,
        b_partner, b_partner_left, b_partner_right, b_partner_far,
    ]
    strip = [rows, below, above, far, s_own, s_below, s_above, s_far]

    m_partner = send(moved, across)
    m_left, m_right = send(moved, forth), send(moved, back)
    half_coupled = row_product(all_blocks, strip, where, row_blocks, True)
    c_below, c_above = send(half_coupled, shift(dy=1)), send(half_coupled, shift(dy=-1))
    where_late, _ = together(where, half_coupled)
    solved = row_product(all_blocks, strip, where_late, row_blocks, False)
    m_partner, m_left, m_right, _ = together(m_partner, m_left, m_right, half_coupled)
    m_far = send(m_left, forth)
    m_partner_right = send(m_partner, back)
    m_partner_left = send(m_left, across)
    solved, c_below, c_above = together(solved, c_below, c_above)
    c_top, c_bottom = together(top(c_below), bottom(c_above))
    c_far = [send(c_top, shift(dy=1)), send(c_bottom, shift(dy=-1))]
    m_top, m_bottom, m_far, half_coupled = together(
        top(m_partner_left), bottom(m_partner_right), m_far, half_coupled
    )
    m_partner_far = [send(m_top, forth), send(m_bottom, back)]
    t_own = send(half_coupled, other_core)
    t_below, t_above, _, *c_far = together(c_below, c_above, m_top, *c_far)
    t_far = [send(part, other_core) for part in c_far]
    t_below, t_above = send(t_below, other_core), send(t_above, other_core)

    lefts = [
        [moved], [m_left], [m_right], [m_far], [m_partner], [m_partner_left], [m_partner_right],
    ]
    own_strip = [[half_coupled], [c_below], [c_above]]
    where_late, *c_far = together(where, *c_far)
    child = block_product(diag_inverse[0], lefts, own_strip, where_late, 3, False)
    child = block_product(
        child,
        lefts + [m_partner_far],
        own_strip + [c_far, [t_own], [t_below], [t_above], t_far],
        where,
        3,
        True,
    )
    return solved[None], child[None]


def solution(mesh):
    return jax.shard_map(
        per_device,
        mesh=mesh,
        in_specs=(P(("gz", "row"), "col"), P(), P("gz", "row", "col"), P("gz", "row", "col")),
        out_specs=(P("gz", "row", "col"), P("gz", "row", "col")),
        check_vma=False,
    )
```

```python
import jax
import jax.numpy as jnp
from jax import lax
from jax.experimental import pallas as pl
from jax.experimental.pallas import tpu as pltpu
from jax.sharding import PartitionSpec as P

AXES = ("gz", "row", "col")
VMEM_BYTES = 62 * 1024 * 1024
SMALL_VMEM_BYTES = 8 * 1024 * 1024
ANY = pl.BlockSpec(memory_space=pl.ANY)
SMEM = pl.BlockSpec(memory_space=pltpu.SMEM)
WHOLE = pl.BlockSpec(memory_space=pltpu.VMEM)


def send(array, place):
    pairs = []
    for gz in range(2):
        for row in range(8):
            for col in range(8):
                x, y, z, core = place(2 * (col // 4) + gz, row // 2, col % 4, row % 2)
                x, y, z = x % 4, y % 4, z % 4
                target = ((x % 2) * 8 + 2 * y + core) * 8 + 4 * (x // 2) + z
                pairs.append(((gz * 8 + row) * 8 + col, target))
    return lax.ppermute(array, AXES, pairs)


def shift(dx=0, dy=0, dz=0, core=0):
    return lambda x, y, z, k: (x + dx, y + dy, z + dz, k ^ core)


def spread_place(x, y, z, core):
    return 2 * ((x // 2) ^ (y // 2)) + x % 2, y, z ^ (2 * (y % 2) + core), core


def row_place(x, y, z, core):
    return x, y ^ (2 * (x // 2) + z // 2), z, core ^ (z % 2)


def column_places(half, z):
    around = [z, (z + 3) & 3, (z + 1) & 3, (z + 2) & 3]
    return [(half, p) for p in around] + [(1 - half, p) for p in around]


def chosen_slots(lists, child, half, z):
    return [2 * p + held_second(lists, child, h, p) for h, p in column_places(half, z)]


def turned_slots(lists, child, row, half, z):
    high = lists[child, row] // 16
    return [2 * (p ^ (row >> 1)) + (h ^ high) for h, p in column_places(half, z)]


def held_second(lists, child, half, z):
    return (lists[child, 2 * z + 1] // 16 == half).astype(jnp.int32)


def panel_slots(row, half, z):
    return [row ^ (4 * h + p) for h, p in column_places(half, z)]


def strip_slots(row):
    y, core = row >> 1, row & 1
    steps = [y, (y + 3) & 3, (y + 1) & 3, (y + 2) & 3]
    return [2 * p + core for p in steps] + [2 * p + 1 - core for p in steps]


def together(*values):
    return lax.optimization_barrier(values)


def params(limit=VMEM_BYTES):
    return pltpu.CompilerParams(vmem_limit_bytes=limit)


def cost(flops, elements):
    return pl.CostEstimate(flops=1, bytes_accessed=1, transcendentals=0)


def halves(value):
    high = value.astype(jnp.bfloat16)
    return high, (value - high.astype(jnp.float32)).astype(jnp.bfloat16)


def product(left, right):
    def one(a, b):
        return jnp.dot(a, b, preferred_element_type=jnp.float32)

    return one(left[0], right[0]) + (one(left[0], right[1]) + one(left[1], right[0]))


def pick(ancestor, row_blocks, where, tile):
    def body(where_ref, lists_ref, ancestor_ref, own_ref, other_ref, held, sems):
        gz, row, half, z = (where_ref[i] for i in range(4))
        copies, holds = [], []
        for i, child in enumerate((gz, 1 - gz)):
            entry = lists_ref[child, row]
            first, second = lists_ref[child, 2 * z], lists_ref[child, 2 * z + 1]
            across = jnp.where(second // 16 == half, second, first)
            copies.append(
                pltpu.make_async_copy(
                    ancestor_ref.at[
                        pl.ds(pl.multiple_of((entry % 2) * tile, tile), tile),
                        pl.ds(pl.multiple_of((across % 4) * tile, tile), tile),
                    ],
                    held.at[i],
                    sems.at[i],
                )
            )
            holds.append(entry // 16 == gz)
        for copy in copies:
            copy.start()
        for i, out_ref in enumerate((own_ref, other_ref)):
            copies[i].wait()

            @pl.when(holds[i])
            def _():
                out_ref[...] = held[i]

            @pl.when(jnp.logical_not(holds[i]))
            def _():
                out_ref[...] = jnp.zeros((tile, tile), jnp.float32)

    return pl.pallas_call(
        body,
        out_shape=[jax.ShapeDtypeStruct((tile, tile), jnp.float32)] * 2,
        in_specs=[SMEM, SMEM, ANY],
        out_specs=[WHOLE] * 2,
        scratch_shapes=[
            pltpu.VMEM((2, tile, tile), jnp.float32),
            pltpu.SemaphoreType.DMA((2,)),
        ],
        compiler_params=params(),
        cost_estimate=cost(0, 4 * tile * tile),
        name="pick",
    )(where, row_blocks, ancestor)


def joined(first, second):
    def body(first_ref, second_ref, out_ref):
        out_ref[...] = first_ref[...] + second_ref[...]

    return pl.pallas_call(
        body,
        out_shape=jax.ShapeDtypeStruct(first.shape, jnp.float32),
        in_specs=[WHOLE] * 2,
        out_specs=WHOLE,
        compiler_params=params(SMALL_VMEM_BYTES),
        cost_estimate=cost(0, 3 * first.size),
        name="joined",
    )(first, second)


def sort_piece(piece, where, row_blocks):
    def body(where_ref, lists_ref, piece_ref, same_ref, other_ref):
        gz, row, half, z = (where_ref[i] for i in range(4))
        core = row & 1
        is_same = held_second(lists_ref, gz, half ^ core, z ^ (row >> 1)) == core

        @pl.when(is_same)
        def _():
            same_ref[...] = piece_ref[...]
            other_ref[...] = jnp.zeros(piece.shape, jnp.float32)

        @pl.when(jnp.logical_not(is_same))
        def _():
            same_ref[...] = jnp.zeros(piece.shape, jnp.float32)
            other_ref[...] = piece_ref[...]

    return pl.pallas_call(
        body,
        out_shape=[jax.ShapeDtypeStruct(piece.shape, jnp.float32)] * 2,
        in_specs=[SMEM, SMEM, WHOLE],
        out_specs=[WHOLE] * 2,
        compiler_params=params(SMALL_VMEM_BYTES),
        cost_estimate=cost(0, 3 * piece.size),
        name="sort_piece",
    )(where, row_blocks, piece)


def turned(block):
    tile, width = block.shape

    def body(block_ref, out_ref):
        out_ref[...] = block_ref[...].T

    return pl.pallas_call(
        body,
        grid=(width // tile,),
        out_shape=jax.ShapeDtypeStruct((width, tile), jnp.float32),
        in_specs=[pl.BlockSpec((tile, tile), lambda i: (0, i))],
        out_specs=pl.BlockSpec((tile, tile), lambda i: (i, 0)),
        compiler_params=params(SMALL_VMEM_BYTES),
        cost_estimate=cost(0, 2 * tile * width),
        name="turned",
    )(block)


def stacked(mine, first, second):
    tile = mine.shape[0]

    def body(mine_ref, first_ref, second_ref, out_ref):
        out_ref[:tile] = mine_ref[...]
        out_ref[tile:] = (first_ref[...] + second_ref[...]).T

    return pl.pallas_call(
        body,
        out_shape=jax.ShapeDtypeStruct((2 * tile, tile), jnp.float32),
        in_specs=[WHOLE] * 3,
        out_specs=WHOLE,
        compiler_params=params(SMALL_VMEM_BYTES),
        cost_estimate=cost(0, 5 * mine.size),
        name="stacked",
    )(mine, first, second)


def group_copies(groups, held, slots, sems):
    copies = []
    for i, group in enumerate(groups):
        start, out = 0, []
        for part, ref in enumerate(group):
            rows = ref.shape[0]
            target = held.at[slots[i], pl.ds(start, rows)]
            out.append(pltpu.make_async_copy(ref, target, sems.at[slots[i], part]))
            start += rows
        copies.append(out)
    return copies


def flat(groups):
    return [part for group in groups for part in group]


def grouped(refs, groups):
    out, start = [], 0
    for group in groups:
        out.append(refs[start : start + len(group)])
        start += len(group)
    return out


def row_product(blocks, strip, where, row_blocks, symmetric):
    count = len(blocks)
    tile, width = blocks[0].shape[1], strip[0].shape[1]
    parts = 2 if symmetric else 1

    def body(where_ref, lists_ref, *refs):
        block_refs, strip_refs = refs[:count], refs[count : 2 * count]
        out_ref, lefts, rights, left_sems, right_sems = refs[2 * count :]
        gz, row, half, z = (where_ref[i] for i in range(4))
        slots = [chosen_slots(lists_ref, gz, half, z), turned_slots(lists_ref, gz, row, half, z)]
        left = [
            pltpu.make_async_copy(
                block_refs[d].at[pl.ds(part * tile, tile)],
                lefts.at[part, slots[part][d]],
                left_sems.at[part, d],
            )
            for part in range(parts)
            for d in range(count)
        ]
        right = [
            pltpu.make_async_copy(strip_refs[i], rights.at[i], right_sems.at[i])
            for i in range(count)
        ]
        for copy in left + right[:2]:
            copy.start()
        for copy in left:
            copy.wait()
        for i, slot in enumerate(strip_slots(row)):
            right[i].wait()
            if i + 2 < count:
                right[i + 2].start()
            block = 0.5 * (lefts[0, slot] + lefts[1, slot]) if symmetric else -lefts[0, slot]
            term = product(halves(block), halves(rights[i]))
            if i == 0:
                out_ref[...] = term
            else:
                out_ref[...] += term

    return pl.pallas_call(
        body,
        out_shape=jax.ShapeDtypeStruct((tile, width), jnp.float32),
        in_specs=[SMEM, SMEM] + [ANY] * (2 * count),
        out_specs=WHOLE,
        scratch_shapes=[
            pltpu.VMEM((parts, count, tile, tile), jnp.float32),
            pltpu.VMEM((count, tile, width), jnp.float32),
            pltpu.SemaphoreType.DMA((parts, count)),
            pltpu.SemaphoreType.DMA((count,)),
        ],
        compiler_params=params(),
        cost_estimate=cost(6 * count * tile * tile * width, (count + 2) * tile * (width + tile)),
        name="row_product",
    )(where, row_blocks, *blocks, *strip)


def block_product(base, lefts, strip, where, first_late, late):
    count, rights = len(lefts), len(strip)
    left_pieces, strip_pieces = len(flat(lefts)), len(flat(strip))
    tile = lefts[0][0].shape[1]
    width = strip[0][0].shape[1]
    ahead = 3
    arrays = [part[0] if isinstance(part, tuple) else part for part in flat(strip)]

    def body(where_ref, base_ref, *refs):
        left_refs = grouped(refs[:left_pieces], lefts)
        refs = refs[left_pieces:]
        views = [
            ref.at[pl.ds(part[1] * tile, tile)] if isinstance(part, tuple) else ref
            for ref, part in zip(refs[:strip_pieces], flat(strip))
        ]
        strip_refs = grouped(views, strip)
        (
            out_ref, total, base_held, left_held, right_held,
            base_sem, left_sems, right_sems, out_sems,
        ) = refs[strip_pieces:]
        row, half, z = (where_ref[i] for i in (1, 2, 3))
        left_slots, right_slots = panel_slots(row, half, z), strip_slots(row)
        late_slots = right_slots[first_late:] + left_slots[7:]

        def used(slot):
            found = slot == late_slots[0]
            for other in late_slots[1:]:
                found = jnp.logical_or(found, slot == other)
            return found if late else jnp.logical_not(found)

        base_copy = pltpu.make_async_copy(base_ref, base_held, base_sem.at[0])
        left = group_copies(left_refs, left_held, list(range(count)), left_sems)

        def right_copies(d):
            return group_copies(strip_refs, right_held, [d] * rights, right_sems)

        def matching(d, act):
            for i, copies in enumerate(right_copies(d)):

                @pl.when(jnp.logical_and(used(left_slots[d]), right_slots[i] == left_slots[d]))
                def _():
                    for copy in copies:
                        act(copy)

        def fetch(d):
            matching(d, lambda copy: copy.start())

            @pl.when(used(left_slots[d]))
            def _():
                for copy in left[d]:
                    copy.start()

        for d in range(min(ahead, count)):
            fetch(d)
        total[...] = jnp.zeros_like(total)
        for d in range(count):
            if d + ahead < count:
                fetch(d + ahead)
            if d + ahead == count:
                base_copy.start()
            matching(d, lambda copy: copy.wait())

            @pl.when(used(left_slots[d]))
            def _():
                for copy in left[d]:
                    copy.wait()
                right_parts = halves(right_held[d])
                for t in range(0, width, tile):
                    rows = pl.ds(t, tile)
                    total[rows, :] += product(halves(left_held[d, rows, :]), right_parts)

        base_copy.wait()
        results = []
        for t in range(0, width, tile):
            rows = pl.ds(t, tile)
            total[rows, :] += base_held[rows, :]
            results.append(
                pltpu.make_async_copy(total.at[rows], out_ref.at[rows], out_sems.at[t // tile])
            )
            results[-1].start()
        for copy in results:
            copy.wait()

    return pl.pallas_call(
        body,
        out_shape=jax.ShapeDtypeStruct((width, width), jnp.float32),
        in_specs=[SMEM] + [ANY] * (1 + left_pieces + strip_pieces),
        out_specs=ANY,
        scratch_shapes=[
            pltpu.VMEM((width, width), jnp.float32),
            pltpu.VMEM((width, width), jnp.float32),
            pltpu.VMEM((count, width, tile), jnp.float32),
            pltpu.VMEM((8, tile, width), jnp.float32),
            pltpu.SemaphoreType.DMA((1,)),
            pltpu.SemaphoreType.DMA((count, 2)),
            pltpu.SemaphoreType.DMA((8, 2)),
            pltpu.SemaphoreType.DMA((width // tile,)),
        ],
        compiler_params=params(),
        cost_estimate=cost(
            6 * count * tile * width * width, 2 * width * width + 2 * count * tile * width
        ),
        name="block_product",
    )(where, base, *flat(lefts), *arrays)


def copied(outputs):
    parts = flat(outputs)
    shapes = [
        jax.ShapeDtypeStruct((sum(rows for _, _, rows in out), out[0][0].shape[1]), jnp.float32)
        for out in outputs
    ]

    def body(*refs):
        in_refs, out_refs = refs[: len(parts)], refs[len(parts) : len(parts) + len(shapes)]
        held, sems = refs[len(parts) + len(shapes) : -1], refs[-1]
        copies = []
        for out_ref, out in zip(out_refs, outputs):
            at = 0
            for _, start, rows in out:
                i = len(copies)
                source, target = in_refs[i].at[pl.ds(start, rows)], out_ref.at[pl.ds(at, rows)]
                copies.append(
                    (
                        pltpu.make_async_copy(source, held[i], sems.at[i, 0]),
                        pltpu.make_async_copy(held[i], target, sems.at[i, 1]),
                    )
                )
                at += rows
        for first, _ in copies:
            first.start()
        for first, second in copies:
            first.wait()
            second.start()
        for _, second in copies:
            second.wait()

    return pl.pallas_call(
        body,
        out_shape=shapes,
        in_specs=[ANY] * len(parts),
        out_specs=[ANY] * len(shapes),
        scratch_shapes=[pltpu.VMEM((rows, array.shape[1]), jnp.float32) for array, _, rows in parts]
        + [pltpu.SemaphoreType.DMA((len(parts), 2))],
        compiler_params=params(),
        cost_estimate=cost(0, 0),
        name="copied",
    )(*[array for array, _, _ in parts])


def per_device(anc_inverse, row_blocks, panel, diag_inverse):
    rows = panel[0]
    tile = rows.shape[0]
    gz, row, col = (lax.axis_index(name) for name in AXES)
    where = jnp.stack([gz, row, col // 4, col % 4])
    other_core, across, back, forth = shift(core=1), shift(dx=2), shift(dz=-1), shift(dz=1)

    below, above = send(rows, shift(dy=1)), send(rows, shift(dy=-1))
    own, other = pick(anc_inverse, row_blocks, where, tile)
    mine = joined(own, send(other, lambda x, y, z, k: (x ^ 1, y, z, k)))
    piece = send(mine, lambda x, y, z, k: (x ^ (2 * k), y, z ^ y, k))
    same, other = sort_piece(piece, where, row_blocks)
    rows_turned = turned(rows)
    s_own = send(rows, other_core)
    rows, mine, same, other, below, above, s_own, rows_turned = together(
        rows, mine, same, other, below, above, s_own, rows_turned
    )

    same = send(same, lambda x, y, z, k: (x, y ^ z, z, k))
    other = send(other, lambda x, y, z, k: (x, y ^ z, z, k ^ 1))
    spread = send(rows_turned, spread_place)
    s_below, s_above = send(below, other_core), send(above, other_core)
    blocks = stacked(mine, same, other)
    rows, blocks, s_below, s_above = together(rows, blocks, s_below, s_above)

    b_left, b_right = send(blocks, forth), send(blocks, back)
    b_far, b_partner = send(blocks, shift(dz=2)), send(blocks, across)
    far = send(rows, shift(dy=2))
    spread, _ = together(spread, b_left)
    moved = send(spread, row_place)
    b_left, b_right, b_far, b_partner, far = together(b_left, b_right, b_far, b_partner, far)
    b_partner_left, b_partner_right = send(b_partner, forth), send(b_partner, back)
    b_partner_far = send(b_far, across)
    s_far = send(far, other_core)
    moved, b_partner_left, b_partner_right, b_partner_far, s_far = together(
        moved, b_partner_left, b_partner_right, b_partner_far, s_far
    )
    all_blocks = [
        blocks, b_left, b_right, b_far,
        b_partner, b_partner_left, b_partner_right, b_partner_far,
    ]
    strip = [rows, below, above, far, s_own, s_below, s_above, s_far]

    m_partner = send(moved, across)
    m_left, m_right = send(moved, forth), send(moved, back)
    half_coupled = row_product(all_blocks, strip, where, row_blocks, True)
    c_below, c_above = send(half_coupled, shift(dy=1)), send(half_coupled, shift(dy=-1))
    where_late, _ = together(where, half_coupled)
    solved = row_product(all_blocks, strip, where_late, row_blocks, False)
    m_partner, m_left, m_right, _ = together(m_partner, m_left, m_right, half_coupled)
    m_far = send(m_left, forth)
    m_partner_right = send(m_partner, back)
    m_partner_left = send(m_left, across)
    solved, c_below, c_above = together(solved, c_below, c_above)
    mid = tile // 2
    c_top, c_bottom = copied([[(c_below, 0, mid)], [(c_above, mid, mid)]])
    c_far = [send(c_top, shift(dy=1)), send(c_bottom, shift(dy=-1))]
    (piled,) = copied([[(part, 0, tile) for part in (half_coupled, c_below, c_above)]])
    mid = m_partner_left.shape[0] // 2
    m_top, m_bottom = copied([[(m_partner_left, 0, mid)], [(m_partner_right, mid, mid)]])
    m_top, m_bottom, m_far = together(m_top, m_bottom, m_far)
    m_partner_far = [send(m_top, forth), send(m_bottom, back)]
    m_far, *c_far = together(m_far, *c_far)

    lefts = [
        [moved], [m_left], [m_right], [m_far], [m_partner], [m_partner_left], [m_partner_right],
    ]
    own_strip = [[half_coupled], [c_below], [c_above], c_far]
    child = block_product(diag_inverse[0], lefts, own_strip, where, 4, False)
    piled, _, *t_far = together(piled, m_top, *c_far)
    piled, *t_far = [send(part, other_core) for part in (piled, *t_far)]
    child = block_product(
        child,
        lefts + [m_partner_far],
        own_strip + [[(piled, 0)], [(piled, 1)], [(piled, 2)], t_far],
        where,
        4,
        True,
    )
    return solved[None], child[None]


def solution(mesh):
    return jax.shard_map(
        per_device,
        mesh=mesh,
        in_specs=(P(("gz", "row"), "col"), P(), P("gz", "row", "col"), P("gz", "row", "col")),
        out_specs=(P("gz", "row", "col"), P("gz", "row", "col")),
        check_vma=False,
    )
```

```python
import jax
import jax.numpy as jnp
from jax import lax
from jax.experimental import pallas as pl
from jax.experimental.pallas import tpu as pltpu
from jax.sharding import PartitionSpec as P

AXES = ("gz", "row", "col")
VMEM_BYTES = 62 * 1024 * 1024
SMALL_VMEM_BYTES = 8 * 1024 * 1024
ANY = pl.BlockSpec(memory_space=pl.ANY)
SMEM = pl.BlockSpec(memory_space=pltpu.SMEM)
WHOLE = pl.BlockSpec(memory_space=pltpu.VMEM)


def send(array, place):
    pairs = []
    for gz in range(2):
        for row in range(8):
            for col in range(8):
                x, y, z, core = place(2 * (col // 4) + gz, row // 2, col % 4, row % 2)
                x, y, z = x % 4, y % 4, z % 4
                target = ((x % 2) * 8 + 2 * y + core) * 8 + 4 * (x // 2) + z
                pairs.append(((gz * 8 + row) * 8 + col, target))
    return lax.ppermute(array, AXES, pairs)


def shift(dx=0, dy=0, dz=0, core=0):
    return lambda x, y, z, k: (x + dx, y + dy, z + dz, k ^ core)


def spread_place(x, y, z, core):
    return 2 * ((x // 2) ^ (y // 2)) + x % 2, y, z ^ (2 * (y % 2) + core), core


def row_place(x, y, z, core):
    return x, y ^ (2 * (x // 2) + z // 2), z, core ^ (z % 2)


def column_places(half, z):
    around = [z, (z + 3) & 3, (z + 1) & 3, (z + 2) & 3]
    return [(half, p) for p in around] + [(1 - half, p) for p in around]


def chosen_slots(lists, child, half, z):
    return [2 * p + held_second(lists, child, h, p) for h, p in column_places(half, z)]


def turned_slots(lists, child, row, half, z):
    high = lists[child, row] // 16
    return [2 * (p ^ (row >> 1)) + (h ^ high) for h, p in column_places(half, z)]


def held_second(lists, child, half, z):
    return (lists[child, 2 * z + 1] // 16 == half).astype(jnp.int32)


def panel_slots(row, half, z):
    return [row ^ (4 * h + p) for h, p in column_places(half, z)]


def strip_slots(row):
    y, core = row >> 1, row & 1
    steps = [y, (y + 3) & 3, (y + 1) & 3, (y + 2) & 3]
    return [2 * p + core for p in steps] + [2 * p + 1 - core for p in steps]


def together(*values):
    return lax.optimization_barrier(values)


def params(limit=VMEM_BYTES):
    return pltpu.CompilerParams(vmem_limit_bytes=limit)


def cost(flops, elements):
    return pl.CostEstimate(flops=1, bytes_accessed=1, transcendentals=0)


def halves(value):
    high = value.astype(jnp.bfloat16)
    return high, (value - high.astype(jnp.float32)).astype(jnp.bfloat16)


def product(left, right):
    def one(a, b):
        return jnp.dot(a, b, preferred_element_type=jnp.float32)

    return one(left[0], right[0]) + (one(left[0], right[1]) + one(left[1], right[0]))


def pick(ancestor, row_blocks, where, tile):
    def body(where_ref, lists_ref, ancestor_ref, own_ref, other_ref, held, sems):
        gz, row, half, z = (where_ref[i] for i in range(4))
        copies, holds = [], []
        for i, child in enumerate((gz, 1 - gz)):
            entry = lists_ref[child, row]
            first, second = lists_ref[child, 2 * z], lists_ref[child, 2 * z + 1]
            across = jnp.where(second // 16 == half, second, first)
            copies.append(
                pltpu.make_async_copy(
                    ancestor_ref.at[
                        pl.ds(pl.multiple_of((entry % 2) * tile, tile), tile),
                        pl.ds(pl.multiple_of((across % 4) * tile, tile), tile),
                    ],
                    held.at[i],
                    sems.at[i],
                )
            )
            holds.append(entry // 16 == gz)
        for copy in copies:
            copy.start()
        for i, out_ref in enumerate((own_ref, other_ref)):
            copies[i].wait()

            @pl.when(holds[i])
            def _():
                out_ref[...] = held[i]

            @pl.when(jnp.logical_not(holds[i]))
            def _():
                out_ref[...] = jnp.zeros((tile, tile), jnp.float32)

    return pl.pallas_call(
        body,
        out_shape=[jax.ShapeDtypeStruct((tile, tile), jnp.float32)] * 2,
        in_specs=[SMEM, SMEM, ANY],
        out_specs=[WHOLE] * 2,
        scratch_shapes=[
            pltpu.VMEM((2, tile, tile), jnp.float32),
            pltpu.SemaphoreType.DMA((2,)),
        ],
        compiler_params=params(),
        cost_estimate=cost(0, 4 * tile * tile),
        name="pick",
    )(where, row_blocks, ancestor)


def joined(first, second):
    def body(first_ref, second_ref, out_ref):
        out_ref[...] = first_ref[...] + second_ref[...]

    return pl.pallas_call(
        body,
        out_shape=jax.ShapeDtypeStruct(first.shape, jnp.float32),
        in_specs=[WHOLE] * 2,
        out_specs=WHOLE,
        compiler_params=params(SMALL_VMEM_BYTES),
        cost_estimate=cost(0, 3 * first.size),
        name="joined",
    )(first, second)


def sort_piece(piece, where, row_blocks):
    def body(where_ref, lists_ref, piece_ref, same_ref, other_ref):
        gz, row, half, z = (where_ref[i] for i in range(4))
        core = row & 1
        is_same = held_second(lists_ref, gz, half ^ core, z ^ (row >> 1)) == core

        @pl.when(is_same)
        def _():
            same_ref[...] = piece_ref[...]
            other_ref[...] = jnp.zeros(piece.shape, jnp.float32)

        @pl.when(jnp.logical_not(is_same))
        def _():
            same_ref[...] = jnp.zeros(piece.shape, jnp.float32)
            other_ref[...] = piece_ref[...]

    return pl.pallas_call(
        body,
        out_shape=[jax.ShapeDtypeStruct(piece.shape, jnp.float32)] * 2,
        in_specs=[SMEM, SMEM, WHOLE],
        out_specs=[WHOLE] * 2,
        compiler_params=params(SMALL_VMEM_BYTES),
        cost_estimate=cost(0, 3 * piece.size),
        name="sort_piece",
    )(where, row_blocks, piece)


def turned(block):
    tile, width = block.shape

    def body(block_ref, out_ref):
        out_ref[...] = block_ref[...].T

    return pl.pallas_call(
        body,
        grid=(width // tile,),
        out_shape=jax.ShapeDtypeStruct((width, tile), jnp.float32),
        in_specs=[pl.BlockSpec((tile, tile), lambda i: (0, i))],
        out_specs=pl.BlockSpec((tile, tile), lambda i: (i, 0)),
        compiler_params=params(SMALL_VMEM_BYTES),
        cost_estimate=cost(0, 2 * tile * width),
        name="turned",
    )(block)


def stacked(mine, first, second):
    tile = mine.shape[0]

    def body(mine_ref, first_ref, second_ref, out_ref):
        out_ref[:tile] = mine_ref[...]
        out_ref[tile:] = (first_ref[...] + second_ref[...]).T

    return pl.pallas_call(
        body,
        out_shape=jax.ShapeDtypeStruct((2 * tile, tile), jnp.float32),
        in_specs=[WHOLE] * 3,
        out_specs=WHOLE,
        compiler_params=params(SMALL_VMEM_BYTES),
        cost_estimate=cost(0, 5 * mine.size),
        name="stacked",
    )(mine, first, second)


def group_copies(groups, held, slots, sems):
    copies = []
    for i, group in enumerate(groups):
        start, out = 0, []
        for part, ref in enumerate(group):
            rows = ref.shape[0]
            target = held.at[slots[i], pl.ds(start, rows)]
            out.append(pltpu.make_async_copy(ref, target, sems.at[slots[i], part]))
            start += rows
        copies.append(out)
    return copies


def flat(groups):
    return [part for group in groups for part in group]


def grouped(refs, groups):
    out, start = [], 0
    for group in groups:
        out.append(refs[start : start + len(group)])
        start += len(group)
    return out


def row_product(blocks, strip, where, row_blocks, symmetric):
    count = len(blocks)
    tile, width = blocks[0].shape[1], strip[0].shape[1]
    parts = 2 if symmetric else 1

    def body(where_ref, lists_ref, *refs):
        block_refs, strip_refs = refs[:count], refs[count : 2 * count]
        out_ref, lefts, rights, left_sems, right_sems = refs[2 * count :]
        gz, row, half, z = (where_ref[i] for i in range(4))
        slots = [chosen_slots(lists_ref, gz, half, z), turned_slots(lists_ref, gz, row, half, z)]
        left = [
            pltpu.make_async_copy(
                block_refs[d].at[pl.ds(part * tile, tile)],
                lefts.at[part, slots[part][d]],
                left_sems.at[part, slots[part][d]],
            )
            for part in range(parts)
            for d in range(count)
        ]
        right = [
            pltpu.make_async_copy(strip_refs[i], rights.at[i], right_sems.at[i])
            for i in range(count)
        ]
        right[0].start()
        for copy in left:
            copy.start()
        right[1].start()
        for i, slot in enumerate(strip_slots(row)):
            for part in range(parts):
                pltpu.make_async_copy(
                    block_refs[0].at[pl.ds(0, tile)],
                    lefts.at[part, slot],
                    left_sems.at[part, slot],
                ).wait()
            right[i].wait()
            if i + 2 < count:
                right[i + 2].start()
            block = 0.5 * (lefts[0, slot] + lefts[1, slot]) if symmetric else -lefts[0, slot]
            term = product(halves(block), halves(rights[i]))
            if i == 0:
                out_ref[...] = term
            else:
                out_ref[...] += term

    return pl.pallas_call(
        body,
        out_shape=jax.ShapeDtypeStruct((tile, width), jnp.float32),
        in_specs=[SMEM, SMEM] + [ANY] * (2 * count),
        out_specs=WHOLE,
        scratch_shapes=[
            pltpu.VMEM((parts, count, tile, tile), jnp.float32),
            pltpu.VMEM((count, tile, width), jnp.float32),
            pltpu.SemaphoreType.DMA((parts, count)),
            pltpu.SemaphoreType.DMA((count,)),
        ],
        compiler_params=params(),
        cost_estimate=cost(6 * count * tile * tile * width, (count + 2) * tile * (width + tile)),
        name="row_product",
    )(where, row_blocks, *blocks, *strip)


def block_product(base, lefts, strip, where, first_late, late):
    count, rights = len(lefts), len(strip)
    left_pieces, strip_pieces = len(flat(lefts)), len(flat(strip))
    tile = lefts[0][0].shape[1]
    width = strip[0][0].shape[1]
    ahead = 3
    arrays = [part[0] if isinstance(part, tuple) else part for part in flat(strip)]

    def body(where_ref, base_ref, *refs):
        left_refs = grouped(refs[:left_pieces], lefts)
        refs = refs[left_pieces:]
        views = [
            ref.at[pl.ds(part[1] * tile, tile)] if isinstance(part, tuple) else ref
            for ref, part in zip(refs[:strip_pieces], flat(strip))
        ]
        strip_refs = grouped(views, strip)
        (
            out_ref, total, base_held, left_held, right_held,
            base_sem, left_sems, right_sems, out_sems,
        ) = refs[strip_pieces:]
        row, half, z = (where_ref[i] for i in (1, 2, 3))
        left_slots, right_slots = panel_slots(row, half, z), strip_slots(row)
        late_slots = right_slots[first_late:] + left_slots[7:]

        def used(slot):
            found = slot == late_slots[0]
            for other in late_slots[1:]:
                found = jnp.logical_or(found, slot == other)
            return found if late else jnp.logical_not(found)

        base_copy = pltpu.make_async_copy(base_ref, base_held, base_sem.at[0])
        left = group_copies(left_refs, left_held, list(range(count)), left_sems)

        def right_copies(d):
            return group_copies(strip_refs, right_held, [d] * rights, right_sems)

        def matching(d, act):
            for i, copies in enumerate(right_copies(d)):

                @pl.when(jnp.logical_and(used(left_slots[d]), right_slots[i] == left_slots[d]))
                def _():
                    for copy in copies:
                        act(copy)

        def fetch(d):
            matching(d, lambda copy: copy.start())

            @pl.when(used(left_slots[d]))
            def _():
                for copy in left[d]:
                    copy.start()

        for d in range(min(ahead, count)):
            fetch(d)
        total[...] = jnp.zeros_like(total)
        for d in range(count):
            if d + ahead < count:
                fetch(d + ahead)
            if d + ahead == count:
                base_copy.start()
            matching(d, lambda copy: copy.wait())

            @pl.when(used(left_slots[d]))
            def _():
                for copy in left[d]:
                    copy.wait()
                right_parts = halves(right_held[d])
                for t in range(0, width, tile):
                    rows = pl.ds(t, tile)
                    total[rows, :] += product(halves(left_held[d, rows, :]), right_parts)

        base_copy.wait()
        results = []
        for t in range(0, width, tile):
            rows = pl.ds(t, tile)
            total[rows, :] += base_held[rows, :]
            results.append(
                pltpu.make_async_copy(total.at[rows], out_ref.at[rows], out_sems.at[t // tile])
            )
            results[-1].start()
        for copy in results:
            copy.wait()

    return pl.pallas_call(
        body,
        out_shape=jax.ShapeDtypeStruct((width, width), jnp.float32),
        in_specs=[SMEM] + [ANY] * (1 + left_pieces + strip_pieces),
        out_specs=ANY,
        scratch_shapes=[
            pltpu.VMEM((width, width), jnp.float32),
            pltpu.VMEM((width, width), jnp.float32),
            pltpu.VMEM((count, width, tile), jnp.float32),
            pltpu.VMEM((8, tile, width), jnp.float32),
            pltpu.SemaphoreType.DMA((1,)),
            pltpu.SemaphoreType.DMA((count, 2)),
            pltpu.SemaphoreType.DMA((8, 2)),
            pltpu.SemaphoreType.DMA((width // tile,)),
        ],
        compiler_params=params(),
        cost_estimate=cost(
            6 * count * tile * width * width, 2 * width * width + 2 * count * tile * width
        ),
        name="block_product",
    )(where, base, *flat(lefts), *arrays)


def copied(outputs):
    parts = flat(outputs)
    shapes = [
        jax.ShapeDtypeStruct((sum(rows for _, _, rows in out), out[0][0].shape[1]), jnp.float32)
        for out in outputs
    ]

    def body(*refs):
        in_refs, out_refs = refs[: len(parts)], refs[len(parts) : len(parts) + len(shapes)]
        held, sems = refs[len(parts) + len(shapes) : -1], refs[-1]
        copies = []
        for out_ref, out in zip(out_refs, outputs):
            at = 0
            for _, start, rows in out:
                i = len(copies)
                source, target = in_refs[i].at[pl.ds(start, rows)], out_ref.at[pl.ds(at, rows)]
                copies.append(
                    (
                        pltpu.make_async_copy(source, held[i], sems.at[i, 0]),
                        pltpu.make_async_copy(held[i], target, sems.at[i, 1]),
                    )
                )
                at += rows
        for first, _ in copies:
            first.start()
        for first, second in copies:
            first.wait()
            second.start()
        for _, second in copies:
            second.wait()

    return pl.pallas_call(
        body,
        out_shape=shapes,
        in_specs=[ANY] * len(parts),
        out_specs=[ANY] * len(shapes),
        scratch_shapes=[pltpu.VMEM((rows, array.shape[1]), jnp.float32) for array, _, rows in parts]
        + [pltpu.SemaphoreType.DMA((len(parts), 2))],
        compiler_params=params(),
        cost_estimate=cost(0, 0),
        name="copied",
    )(*[array for array, _, _ in parts])


def per_device(anc_inverse, row_blocks, panel, diag_inverse):
    rows = panel[0]
    tile = rows.shape[0]
    gz, row, col = (lax.axis_index(name) for name in AXES)
    where = jnp.stack([gz, row, col // 4, col % 4])
    other_core, across, back, forth = shift(core=1), shift(dx=2), shift(dz=-1), shift(dz=1)

    below, above = send(rows, shift(dy=1)), send(rows, shift(dy=-1))
    own, other = pick(anc_inverse, row_blocks, where, tile)
    mine = joined(own, send(other, lambda x, y, z, k: (x ^ 1, y, z, k)))
    piece = send(mine, lambda x, y, z, k: (x ^ (2 * k), y, z ^ y, k))
    same, other = sort_piece(piece, where, row_blocks)
    rows_turned = turned(rows)
    s_own = send(rows, other_core)
    rows, mine, same, other, below, above, s_own, rows_turned = together(
        rows, mine, same, other, below, above, s_own, rows_turned
    )

    same = send(same, lambda x, y, z, k: (x, y ^ z, z, k))
    other = send(other, lambda x, y, z, k: (x, y ^ z, z, k ^ 1))
    spread = send(rows_turned, spread_place)
    s_below, s_above = send(below, other_core), send(above, other_core)
    blocks = stacked(mine, same, other)
    rows, blocks, s_below, s_above = together(rows, blocks, s_below, s_above)

    b_left, b_right = send(blocks, forth), send(blocks, back)
    b_far, b_partner = send(blocks, shift(dz=2)), send(blocks, across)
    far = send(rows, shift(dy=2))
    spread, _ = together(spread, b_left)
    moved = send(spread, row_place)
    b_left, b_right, b_far, b_partner, far = together(b_left, b_right, b_far, b_partner, far)
    b_partner_left, b_partner_right = send(b_partner, forth), send(b_partner, back)
    b_partner_far = send(b_far, across)
    s_far = send(far, other_core)
    moved, b_partner_left, b_partner_right, b_partner_far, s_far = together(
        moved, b_partner_left, b_partner_right, b_partner_far, s_far
    )
    all_blocks = [
        blocks, b_left, b_right, b_far,
        b_partner, b_partner_left, b_partner_right, b_partner_far,
    ]
    strip = [rows, below, above, far, s_own, s_below, s_above, s_far]

    m_partner = send(moved, across)
    m_left, m_right = send(moved, forth), send(moved, back)
    half_coupled = row_product(all_blocks, strip, where, row_blocks, True)
    c_below, c_above = send(half_coupled, shift(dy=1)), send(half_coupled, shift(dy=-1))
    where_late, _ = together(where, half_coupled)
    solved = row_product(all_blocks, strip, where_late, row_blocks, False)
    m_partner, m_left, m_right, _ = together(m_partner, m_left, m_right, half_coupled)
    m_far = send(m_left, forth)
    m_partner_right = send(m_partner, back)
    m_partner_left = send(m_left, across)
    solved, c_below, c_above = together(solved, c_below, c_above)
    mid = tile // 2
    c_top, c_bottom = copied([[(c_below, 0, mid)], [(c_above, mid, mid)]])
    c_far = [send(c_top, shift(dy=1)), send(c_bottom, shift(dy=-1))]
    (piled,) = copied([[(part, 0, tile) for part in (half_coupled, c_below, c_above)]])
    mid = m_partner_left.shape[0] // 2
    m_top, m_bottom = copied([[(m_partner_left, 0, mid)], [(m_partner_right, mid, mid)]])
    m_top, m_bottom, m_far = together(m_top, m_bottom, m_far)
    m_partner_far = [send(m_top, forth), send(m_bottom, back)]
    m_far, *c_far = together(m_far, *c_far)

    lefts = [
        [moved], [m_left], [m_right], [m_far], [m_partner], [m_partner_left], [m_partner_right],
    ]
    own_strip = [[half_coupled], [c_below], [c_above], c_far]
    child = block_product(diag_inverse[0], lefts, own_strip, where, 4, False)
    piled, *t_far = [send(part, other_core) for part in (piled, *c_far)]
    child = block_product(
        child,
        lefts + [m_partner_far],
        own_strip + [[(piled, 0)], [(piled, 1)], [(piled, 2)], t_far],
        where,
        4,
        True,
    )
    return solved[None], child[None]


def solution(mesh):
    return jax.shard_map(
        per_device,
        mesh=mesh,
        in_specs=(P(("gz", "row"), "col"), P(), P("gz", "row", "col"), P("gz", "row", "col")),
        out_specs=(P("gz", "row", "col"), P("gz", "row", "col")),
        check_vma=False,
    )
```

```python
import jax
import jax.numpy as jnp
from jax import lax
from jax.experimental import pallas as pl
from jax.experimental.pallas import tpu as pltpu
from jax.sharding import PartitionSpec as P

AXES = ("gz", "row", "col")
VMEM_BYTES = 62 * 1024 * 1024
SMALL_VMEM_BYTES = 8 * 1024 * 1024
ANY = pl.BlockSpec(memory_space=pl.ANY)
SMEM = pl.BlockSpec(memory_space=pltpu.SMEM)
WHOLE = pl.BlockSpec(memory_space=pltpu.VMEM)


def send(array, place):
    pairs = []
    for gz in range(2):
        for row in range(8):
            for col in range(8):
                x, y, z, core = place(2 * (col // 4) + gz, row // 2, col % 4, row % 2)
                x, y, z = x % 4, y % 4, z % 4
                target = ((x % 2) * 8 + 2 * y + core) * 8 + 4 * (x // 2) + z
                pairs.append(((gz * 8 + row) * 8 + col, target))
    return lax.ppermute(array, AXES, pairs)


def shift(dx=0, dy=0, dz=0, core=0):
    return lambda x, y, z, k: (x + dx, y + dy, z + dz, k ^ core)


def spread_place(x, y, z, core):
    return 2 * ((x // 2) ^ (y // 2)) + x % 2, y, z ^ (2 * (y % 2) + core), core


def row_place(x, y, z, core):
    return x, y ^ (2 * (x // 2) + z // 2), z, core ^ (z % 2)


def column_places(half, z):
    around = [z, (z + 3) & 3, (z + 1) & 3, (z + 2) & 3]
    return [(half, p) for p in around] + [(1 - half, p) for p in around]


def chosen_slots(lists, child, half, z):
    return [2 * p + held_second(lists, child, h, p) for h, p in column_places(half, z)]


def turned_slots(lists, child, row, half, z):
    high = lists[child, row] // 16
    return [2 * (p ^ (row >> 1)) + (h ^ high) for h, p in column_places(half, z)]


def held_second(lists, child, half, z):
    return (lists[child, 2 * z + 1] // 16 == half).astype(jnp.int32)


def panel_slots(row, half, z):
    return [row ^ (4 * h + p) for h, p in column_places(half, z)]


def strip_slots(row):
    y, core = row >> 1, row & 1
    steps = [y, (y + 3) & 3, (y + 1) & 3, (y + 2) & 3]
    return [2 * p + core for p in steps] + [2 * p + 1 - core for p in steps]


def together(*values):
    return lax.optimization_barrier(values)


def params(limit=VMEM_BYTES):
    return pltpu.CompilerParams(vmem_limit_bytes=limit)


def cost(flops, elements):
    return pl.CostEstimate(flops=1, bytes_accessed=1, transcendentals=0)


def halves(value):
    high = value.astype(jnp.bfloat16)
    return high, (value - high.astype(jnp.float32)).astype(jnp.bfloat16)


def product(left, right):
    def one(a, b):
        return jnp.dot(a, b, preferred_element_type=jnp.float32)

    return one(left[0], right[0]) + (one(left[0], right[1]) + one(left[1], right[0]))


def pick(ancestor, row_blocks, where, tile):
    def body(where_ref, lists_ref, ancestor_ref, own_ref, other_ref, held, sems):
        gz, row, half, z = (where_ref[i] for i in range(4))
        copies, holds = [], []
        for i, child in enumerate((gz, 1 - gz)):
            entry = lists_ref[child, row]
            first, second = lists_ref[child, 2 * z], lists_ref[child, 2 * z + 1]
            across = jnp.where(second // 16 == half, second, first)
            copies.append(
                pltpu.make_async_copy(
                    ancestor_ref.at[
                        pl.ds(pl.multiple_of((entry % 2) * tile, tile), tile),
                        pl.ds(pl.multiple_of((across % 4) * tile, tile), tile),
                    ],
                    held.at[i],
                    sems.at[i],
                )
            )
            holds.append(entry // 16 == gz)
        for copy in copies:
            copy.start()
        for i, out_ref in enumerate((own_ref, other_ref)):
            copies[i].wait()

            @pl.when(holds[i])
            def _():
                out_ref[...] = held[i]

            @pl.when(jnp.logical_not(holds[i]))
            def _():
                out_ref[...] = jnp.zeros((tile, tile), jnp.float32)

    return pl.pallas_call(
        body,
        out_shape=[jax.ShapeDtypeStruct((tile, tile), jnp.float32)] * 2,
        in_specs=[SMEM, SMEM, ANY],
        out_specs=[WHOLE] * 2,
        scratch_shapes=[
            pltpu.VMEM((2, tile, tile), jnp.float32),
            pltpu.SemaphoreType.DMA((2,)),
        ],
        compiler_params=params(),
        cost_estimate=cost(0, 4 * tile * tile),
        name="pick",
    )(where, row_blocks, ancestor)


def joined(first, second):
    def body(first_ref, second_ref, out_ref):
        out_ref[...] = first_ref[...] + second_ref[...]

    return pl.pallas_call(
        body,
        out_shape=jax.ShapeDtypeStruct(first.shape, jnp.float32),
        in_specs=[WHOLE] * 2,
        out_specs=WHOLE,
        compiler_params=params(SMALL_VMEM_BYTES),
        cost_estimate=cost(0, 3 * first.size),
        name="joined",
    )(first, second)


def sort_piece(piece, where, row_blocks):
    def body(where_ref, lists_ref, piece_ref, same_ref, other_ref):
        gz, row, half, z = (where_ref[i] for i in range(4))
        core = row & 1
        is_same = held_second(lists_ref, gz, half ^ core, z ^ (row >> 1)) == core

        @pl.when(is_same)
        def _():
            same_ref[...] = piece_ref[...]
            other_ref[...] = jnp.zeros(piece.shape, jnp.float32)

        @pl.when(jnp.logical_not(is_same))
        def _():
            same_ref[...] = jnp.zeros(piece.shape, jnp.float32)
            other_ref[...] = piece_ref[...]

    return pl.pallas_call(
        body,
        out_shape=[jax.ShapeDtypeStruct(piece.shape, jnp.float32)] * 2,
        in_specs=[SMEM, SMEM, WHOLE],
        out_specs=[WHOLE] * 2,
        compiler_params=params(SMALL_VMEM_BYTES),
        cost_estimate=cost(0, 3 * piece.size),
        name="sort_piece",
    )(where, row_blocks, piece)


def turned(block):
    tile, width = block.shape

    def body(block_ref, out_ref):
        out_ref[...] = block_ref[...].T

    return pl.pallas_call(
        body,
        grid=(width // tile,),
        out_shape=jax.ShapeDtypeStruct((width, tile), jnp.float32),
        in_specs=[pl.BlockSpec((tile, tile), lambda i: (0, i))],
        out_specs=pl.BlockSpec((tile, tile), lambda i: (i, 0)),
        compiler_params=params(SMALL_VMEM_BYTES),
        cost_estimate=cost(0, 2 * tile * width),
        name="turned",
    )(block)


def stacked(mine, first, second):
    tile = mine.shape[0]

    def body(mine_ref, first_ref, second_ref, out_ref):
        out_ref[:tile] = mine_ref[...]
        out_ref[tile:] = (first_ref[...] + second_ref[...]).T

    return pl.pallas_call(
        body,
        out_shape=jax.ShapeDtypeStruct((2 * tile, tile), jnp.float32),
        in_specs=[WHOLE] * 3,
        out_specs=WHOLE,
        compiler_params=params(SMALL_VMEM_BYTES),
        cost_estimate=cost(0, 5 * mine.size),
        name="stacked",
    )(mine, first, second)


def group_copies(groups, held, slots, sems):
    copies = []
    for i, group in enumerate(groups):
        start, out = 0, []
        for part, ref in enumerate(group):
            rows = ref.shape[0]
            target = held.at[slots[i], pl.ds(start, rows)]
            out.append(pltpu.make_async_copy(ref, target, sems.at[slots[i], part]))
            start += rows
        copies.append(out)
    return copies


def flat(groups):
    return [part for group in groups for part in group]


def grouped(refs, groups):
    out, start = [], 0
    for group in groups:
        out.append(refs[start : start + len(group)])
        start += len(group)
    return out


def row_product(blocks, strip, where, row_blocks, symmetric):
    count = len(blocks)
    tile, width = blocks[0].shape[1], strip[0].shape[1]
    parts = 2 if symmetric else 1

    def body(where_ref, lists_ref, *refs):
        block_refs, strip_refs = refs[:count], refs[count : 2 * count]
        out_ref, lefts, rights, left_sems, right_sems = refs[2 * count :]
        gz, row, half, z = (where_ref[i] for i in range(4))
        slots = [chosen_slots(lists_ref, gz, half, z), turned_slots(lists_ref, gz, row, half, z)]
        left = [
            pltpu.make_async_copy(
                block_refs[d].at[pl.ds(part * tile, tile)],
                lefts.at[part, slots[part][d]],
                left_sems.at[part, slots[part][d]],
            )
            for part in range(parts)
            for d in range(count)
        ]
        right = [
            pltpu.make_async_copy(strip_refs[i], rights.at[i], right_sems.at[i])
            for i in range(count)
        ]
        right[0].start()
        for copy in left:
            copy.start()
        right[1].start()
        for i, slot in enumerate(strip_slots(row)):
            for part in range(parts):
                pltpu.make_async_copy(
                    block_refs[0].at[pl.ds(0, tile)],
                    lefts.at[part, slot],
                    left_sems.at[part, slot],
                ).wait()
            right[i].wait()
            if i + 2 < count:
                right[i + 2].start()
            block = 0.5 * (lefts[0, slot] + lefts[1, slot]) if symmetric else -lefts[0, slot]
            term = product(halves(block), halves(rights[i]))
            if i == 0:
                out_ref[...] = term
            else:
                out_ref[...] += term

    return pl.pallas_call(
        body,
        out_shape=jax.ShapeDtypeStruct((tile, width), jnp.float32),
        in_specs=[SMEM, SMEM] + [ANY] * (2 * count),
        out_specs=WHOLE,
        scratch_shapes=[
            pltpu.VMEM((parts, count, tile, tile), jnp.float32),
            pltpu.VMEM((count, tile, width), jnp.float32),
            pltpu.SemaphoreType.DMA((parts, count)),
            pltpu.SemaphoreType.DMA((count,)),
        ],
        compiler_params=params(),
        cost_estimate=cost(6 * count * tile * tile * width, (count + 2) * tile * (width + tile)),
        name="row_product",
    )(where, row_blocks, *blocks, *strip)


def block_product(base, lefts, strip, where, first_late, late):
    count, rights = len(lefts), len(strip)
    left_pieces, strip_pieces = len(flat(lefts)), len(flat(strip))
    tile = lefts[0][0].shape[1]
    width = strip[0][0].shape[1]
    ahead = 2
    arrays = [part[0] if isinstance(part, tuple) else part for part in flat(strip)]

    def body(where_ref, base_ref, *refs):
        left_refs = grouped(refs[:left_pieces], lefts)
        refs = refs[left_pieces:]
        views = [
            ref.at[pl.ds(part[1] * tile, tile)] if isinstance(part, tuple) else ref
            for ref, part in zip(refs[:strip_pieces], flat(strip))
        ]
        strip_refs = grouped(views, strip)
        (
            out_ref, total, base_held, left_held, right_held,
            base_sem, left_sems, right_sems, out_sems,
        ) = refs[strip_pieces:]
        row, half, z = (where_ref[i] for i in (1, 2, 3))
        left_slots, right_slots = panel_slots(row, half, z), strip_slots(row)
        late_slots = right_slots[first_late:] + left_slots[7:]

        def used(slot):
            found = slot == late_slots[0]
            for other in late_slots[1:]:
                found = jnp.logical_or(found, slot == other)
            return found if late else jnp.logical_not(found)

        base_copy = pltpu.make_async_copy(base_ref, base_held, base_sem.at[0])
        left = group_copies(left_refs, left_held, list(range(count)), left_sems)

        def right_copies(d):
            return group_copies(strip_refs, right_held, [d] * rights, right_sems)

        def matching(d, act):
            for i, copies in enumerate(right_copies(d)):

                @pl.when(jnp.logical_and(used(left_slots[d]), right_slots[i] == left_slots[d]))
                def _():
                    for copy in copies:
                        act(copy)

        def fetch(d):
            matching(d, lambda copy: copy.start())

            @pl.when(used(left_slots[d]))
            def _():
                for copy in left[d]:
                    copy.start()

        for d in range(min(ahead, count)):
            fetch(d)
        total[...] = jnp.zeros_like(total)
        for d in range(count):
            if d + ahead < count:
                fetch(d + ahead)
            if d + ahead == count:
                base_copy.start()
            matching(d, lambda copy: copy.wait())

            @pl.when(used(left_slots[d]))
            def _():
                for copy in left[d]:
                    copy.wait()
                right_parts = halves(right_held[d])
                for t in range(0, width, tile):
                    rows = pl.ds(t, tile)
                    total[rows, :] += product(halves(left_held[d, rows, :]), right_parts)

        base_copy.wait()
        results = []
        for t in range(0, width, tile):
            rows = pl.ds(t, tile)
            total[rows, :] += base_held[rows, :]
            results.append(
                pltpu.make_async_copy(total.at[rows], out_ref.at[rows], out_sems.at[t // tile])
            )
            results[-1].start()
        for copy in results:
            copy.wait()

    return pl.pallas_call(
        body,
        out_shape=jax.ShapeDtypeStruct((width, width), jnp.float32),
        in_specs=[SMEM] + [ANY] * (1 + left_pieces + strip_pieces),
        out_specs=ANY,
        scratch_shapes=[
            pltpu.VMEM((width, width), jnp.float32),
            pltpu.VMEM((width, width), jnp.float32),
            pltpu.VMEM((count, width, tile), jnp.float32),
            pltpu.VMEM((8, tile, width), jnp.float32),
            pltpu.SemaphoreType.DMA((1,)),
            pltpu.SemaphoreType.DMA((count, 2)),
            pltpu.SemaphoreType.DMA((8, 2)),
            pltpu.SemaphoreType.DMA((width // tile,)),
        ],
        compiler_params=params(),
        cost_estimate=cost(
            6 * count * tile * width * width, 2 * width * width + 2 * count * tile * width
        ),
        name="block_product",
    )(where, base, *flat(lefts), *arrays)


def copied(outputs):
    parts = flat(outputs)
    shapes = [
        jax.ShapeDtypeStruct((sum(rows for _, _, rows in out), out[0][0].shape[1]), jnp.float32)
        for out in outputs
    ]

    def body(*refs):
        in_refs, out_refs = refs[: len(parts)], refs[len(parts) : len(parts) + len(shapes)]
        held, sems = refs[len(parts) + len(shapes) : -1], refs[-1]
        copies = []
        for out_ref, out in zip(out_refs, outputs):
            at = 0
            for _, start, rows in out:
                i = len(copies)
                source, target = in_refs[i].at[pl.ds(start, rows)], out_ref.at[pl.ds(at, rows)]
                copies.append(
                    (
                        pltpu.make_async_copy(source, held[i], sems.at[i, 0]),
                        pltpu.make_async_copy(held[i], target, sems.at[i, 1]),
                    )
                )
                at += rows
        for first, _ in copies:
            first.start()
        for first, second in copies:
            first.wait()
            second.start()
        for _, second in copies:
            second.wait()

    return pl.pallas_call(
        body,
        out_shape=shapes,
        in_specs=[ANY] * len(parts),
        out_specs=[ANY] * len(shapes),
        scratch_shapes=[pltpu.VMEM((rows, array.shape[1]), jnp.float32) for array, _, rows in parts]
        + [pltpu.SemaphoreType.DMA((len(parts), 2))],
        compiler_params=params(),
        cost_estimate=cost(0, 0),
        name="copied",
    )(*[array for array, _, _ in parts])


def per_device(anc_inverse, row_blocks, panel, diag_inverse):
    rows = panel[0]
    tile = rows.shape[0]
    gz, row, col = (lax.axis_index(name) for name in AXES)
    where = jnp.stack([gz, row, col // 4, col % 4])
    other_core, across, back, forth = shift(core=1), shift(dx=2), shift(dz=-1), shift(dz=1)

    below, above = send(rows, shift(dy=1)), send(rows, shift(dy=-1))
    own, other = pick(anc_inverse, row_blocks, where, tile)
    mine = joined(own, send(other, lambda x, y, z, k: (x ^ 1, y, z, k)))
    piece = send(mine, lambda x, y, z, k: (x ^ (2 * k), y, z ^ y, k))
    same, other = sort_piece(piece, where, row_blocks)
    rows_turned = turned(rows)
    s_own = send(rows, other_core)
    rows, mine, same, other, below, above, s_own, rows_turned = together(
        rows, mine, same, other, below, above, s_own, rows_turned
    )

    same = send(same, lambda x, y, z, k: (x, y ^ z, z, k))
    other = send(other, lambda x, y, z, k: (x, y ^ z, z, k ^ 1))
    spread = send(rows_turned, spread_place)
    s_below, s_above = send(below, other_core), send(above, other_core)
    blocks = stacked(mine, same, other)
    rows, blocks, s_below, s_above = together(rows, blocks, s_below, s_above)

    b_left, b_right = send(blocks, forth), send(blocks, back)
    b_far, b_partner = send(blocks, shift(dz=2)), send(blocks, across)
    far = send(rows, shift(dy=2))
    spread, _ = together(spread, b_left)
    moved = send(spread, row_place)
    b_left, b_right, b_far, b_partner, far = together(b_left, b_right, b_far, b_partner, far)
    b_partner_left, b_partner_right = send(b_partner, forth), send(b_partner, back)
    b_partner_far = send(b_far, across)
    s_far = send(far, other_core)
    moved, b_partner_left, b_partner_right, b_partner_far, s_far = together(
        moved, b_partner_left, b_partner_right, b_partner_far, s_far
    )
    all_blocks = [
        blocks, b_left, b_right, b_far,
        b_partner, b_partner_left, b_partner_right, b_partner_far,
    ]
    strip = [rows, below, above, far, s_own, s_below, s_above, s_far]

    m_partner = send(moved, across)
    m_left, m_right = send(moved, forth), send(moved, back)
    half_coupled = row_product(all_blocks, strip, where, row_blocks, True)
    c_below, c_above = send(half_coupled, shift(dy=1)), send(half_coupled, shift(dy=-1))
    where_late, _ = together(where, half_coupled)
    solved = row_product(all_blocks, strip, where_late, row_blocks, False)
    m_partner, m_left, m_right, _ = together(m_partner, m_left, m_right, half_coupled)
    m_far = send(m_left, forth)
    m_partner_right = send(m_partner, back)
    m_partner_left = send(m_left, across)
    solved, c_below, c_above = together(solved, c_below, c_above)
    mid = tile // 2
    c_top, c_bottom = copied([[(c_below, 0, mid)], [(c_above, mid, mid)]])
    c_far = [send(c_top, shift(dy=1)), send(c_bottom, shift(dy=-1))]
    (piled,) = copied([[(part, 0, tile) for part in (half_coupled, c_below, c_above)]])
    mid = m_partner_left.shape[0] // 2
    m_top, m_bottom = copied([[(m_partner_left, 0, mid)], [(m_partner_right, mid, mid)]])
    m_top, m_bottom, m_far = together(m_top, m_bottom, m_far)
    m_partner_far = [send(m_top, forth), send(m_bottom, back)]
    m_far, *c_far = together(m_far, *c_far)

    lefts = [
        [moved], [m_left], [m_right], [m_far], [m_partner], [m_partner_left], [m_partner_right],
    ]
    own_strip = [[half_coupled], [c_below], [c_above], c_far]
    child = block_product(diag_inverse[0], lefts, own_strip, where, 4, False)
    piled, _, *t_far = together(piled, m_top, *c_far)
    piled, *t_far = [send(part, other_core) for part in (piled, *t_far)]
    child = block_product(
        child,
        lefts + [m_partner_far],
        own_strip + [[(piled, 0)], [(piled, 1)], [(piled, 2)], t_far],
        where,
        4,
        True,
    )
    return solved[None], child[None]


def solution(mesh):
    return jax.shard_map(
        per_device,
        mesh=mesh,
        in_specs=(P(("gz", "row"), "col"), P(), P("gz", "row", "col"), P("gz", "row", "col")),
        out_specs=(P("gz", "row", "col"), P("gz", "row", "col")),
        check_vma=False,
    )
```
